32 devices in a mesh: leaf: 8 (over y, x, core), front: 4 (over z).
Axes of the slice: x: 2, y: 2, z: 4, core: 2. Of those that a mesh axis runs over, the one named last changes fastest.
Arguments:
- rhs: bfloat16 [3, 4096, 256], P(None, ('leaf', 'front')), may hold values from -6 to 6
- inverse_blocks: bfloat16 [4096, 3584], P(('leaf', 'front')), may hold values from -0.1875 to 0.1875
- update_blocks: bfloat16 [4096, 1536], P(('leaf', 'front')), may hold values from -0.1875 to 0.1875
- asm_owner: int32 [2, 4096, 1], P(None, ('leaf', 'front')), may hold values from 0 to 7; in each aligned block of 128 rows (0 to 127, 128 to 255, ..., all dimensions but the last counted through in order) at most 64 rows name the same one
- asm_row: int32 [2, 4096], P(None, ('leaf', 'front')), may hold values from 0 to 127
Outputs:
- solutions: float32 [3, 4096, 256], P(None, ('leaf', 'front'))
The draws below stay inside these ranges and needn't reach their ends.
Inputs may be any that keep to these rules, and one draw needn't show every extreme that they name: `asm_owner`: among the 128 update rows of one device at one level (aligned blocks of rows), at most 64 name the same owner, and some block reaches 64.
All inputs are finite; a program needn't handle non-finite values.
Results may differ from the reference program's by a relative error of at most 0.03.
Values may be sent and summed in bfloat16 or wider, within the bound.
No kernel may reach another device: no remote copies, remote signals or barrier semaphores. Data moves between devices by JAX's collectives and lax.ppermute only.
A program may use at most 64 MiB of HBM per device.

```python
import math
import jax
import jax.numpy as jnp
import numpy as np
from jax import lax

PIV_DEV = 128
RHS = 256
LEVELS = 3
SPLIT = 4
BLOCK = 512
ROWS = 4096
CAP = 64


def touch_ends(values, rng, least, top_value):
    index_at = [jax.random.randint(jax.random.fold_in(rng, axis), (), 0, length) for axis, length in enumerate(values.shape)]
    longest = values.shape.index(max(values.shape))
    neighbour = index_at[:longest] + [(index_at[longest] + 1) % values.shape[longest]] + index_at[longest + 1:]
    return values.at[tuple(index_at)].set(least).at[tuple(neighbour)].set(top_value)


def block_levels(stream_key, dims, shards, least, high):
    def one(dim, blocks):
        steps = jax.random.uniform(jax.random.fold_in(jax.random.fold_in(stream_key, 6), dim), (blocks,), jnp.float32, least / len(shards), high / len(shards))
        return jnp.repeat(jnp.exp(steps), dims[dim] // blocks).reshape((-1,) + (1,) * (len(dims) - dim - 1))

    level = one(*shards[0])
    for cut in shards[1:]:
        level = level * one(*cut)
    return level


def shared_out(own_key, own, number, rows, number_of, top, most, skew):
    sequence = jax.random.permutation(own_key, number_of)
    crowded, ordinary = shares(number_of, rows * top, most, skew, True), shares(number_of, rows * top, most, skew, False)
    places = jnp.arange(number_of)

    def named(sizes, rotation):
        used = int((sizes > 0).sum())
        fixed = max(1, used // 4)
        moved = fixed + (places - fixed + rotation * (used - fixed)) % max(1, number_of - fixed)
        return jnp.zeros((number_of,), jnp.int32).at[sequence[jnp.where(places < fixed, places, moved)]].set(jnp.asarray(sizes, jnp.int32))

    sizes = jnp.where(number % 4 == 0, named(crowded, number // 4), named(ordinary, number - number // 4 - 1))
    mixed = jax.random.permutation(jax.random.fold_in(own, 3), number_of)
    giver, taker = mixed[0:number_of // 2 * 2:2], mixed[1:number_of // 2 * 2:2]
    slack = jnp.minimum(sizes[giver] - 1, most - sizes[taker]) // 2
    slack = jnp.where((giver == sequence[0]) | (taker == sequence[0]) | (sizes[taker] == 0), 0, jnp.maximum(slack, 0))
    moved = jax.random.randint(jax.random.fold_in(own, 4), (number_of // 2,), 0, 1 << 20) % (slack + 1)
    sizes = sizes.at[giver].add(-moved).at[taker].add(moved)
    items = jnp.searchsorted(jnp.cumsum(sizes), jnp.arange(rows * top), side="right").astype(jnp.int32)
    table = items.reshape(top, rows).T
    table = table[jax.random.permutation(jax.random.fold_in(own, 1), rows)]
    rotation = jax.random.randint(jax.random.fold_in(own, 2), (rows, 1), 0, top)
    return jnp.take_along_axis(table, (jnp.arange(top)[None, :] + rotation) % top, axis=1)


def shares(amount, total, bound, slope, full):
    loads = [(1 << 20) // math.isqrt(grade ** slope) + 1 for grade in range(1, amount + 1)]
    largest = bound if full else min(bound, max(-(-total // amount), total * loads[0] // sum(loads)))
    least = 1 if total - largest >= amount - 1 else 0
    holding, rest = [largest] + [least] * (amount - 1), total - largest - least * (amount - 1)
    while rest > 0:
        candidates = [i for i in range(1, amount) if holding[i] < largest] or [i for i in range(1, amount) if holding[i] < bound]
        pool, budget = sum([loads[i] for i in candidates]), rest
        for i in candidates:
            more = min(bound - holding[i], max(1, budget * loads[i] // pool), rest)
            holding[i] = holding[i] + more
            rest = rest - more
    return np.array(holding)


def normal_values(rng, extent, spread, bound, cuts=(), kind=jnp.bfloat16):
    loudness = block_levels(rng, extent, cuts, -0.22, 0.18) if cuts else 1.0
    array = jax.random.normal(rng, extent, jnp.float32) * spread * loudness
    return jnp.minimum(jnp.maximum(array, -bound), bound).astype(kind)


def setup_inputs(seed: int = 0) -> dict:
    arg_keys = jax.random.split(jax.random.key(seed), 6)
    rhs = normal_values(arg_keys[0], (LEVELS, ROWS, RHS), 1.0, 6.0, ((1, 32),))
    inverse_blocks = normal_values(arg_keys[1], (ROWS, BLOCK * (2 ** LEVELS - 1)), (2 * BLOCK) ** -0.5, 0.1875, ((0, 32),))
    update_blocks = normal_values(arg_keys[2], (ROWS, BLOCK * (2 ** (LEVELS - 1) - 1)), (2 * BLOCK) ** -0.5, 0.1875, ((0, 32),))
    asm_owner_keys = jax.random.split(jax.random.fold_in(arg_keys[3], 1), (LEVELS - 1) * ROWS // PIV_DEV)
    asm_owner_turns = jax.random.permutation(jax.random.fold_in(arg_keys[3], 3), (LEVELS - 1) * ROWS // PIV_DEV)
    asm_owner = jax.vmap(lambda own, number: shared_out(jax.random.fold_in(arg_keys[3], 2), own, number, PIV_DEV, 2 * SPLIT, 1, CAP, 1))(asm_owner_keys, asm_owner_turns).reshape((LEVELS - 1, ROWS, 1))
    asm_row = touch_ends(jax.random.randint(arg_keys[4], (LEVELS - 1, ROWS), 0, PIV_DEV), jax.random.fold_in(arg_keys[4], 1), 0, PIV_DEV - 1).astype(jnp.int32)
    return {"rhs": rhs, "inverse_blocks": inverse_blocks, "update_blocks": update_blocks, "asm_owner": asm_owner, "asm_row": asm_row}


def apply_blocks(matrix, vectors, front_rows):
    front_total = vectors.shape[0] // front_rows
    stacked = (matrix.reshape(front_total, front_rows, front_rows), vectors.reshape(front_total, front_rows, vectors.shape[1]))
    result = lax.map(lambda paired: jnp.dot(paired[0], paired[1], preferred_element_type=jnp.float32), stacked)
    return result.reshape(vectors.shape[0], vectors.shape[1])


def apply_transposed(matrix, vectors, front_rows):
    front_total = vectors.shape[0] // front_rows
    stacked = (matrix.reshape(front_total, front_rows, front_rows), vectors.reshape(front_total, front_rows, vectors.shape[1]))
    result = lax.map(lambda paired: lax.dot_general(paired[0], paired[1], (((0,), (0,)), ((), ())), preferred_element_type=jnp.float32), stacked)
    return result.reshape(vectors.shape[0], vectors.shape[1])


def reference(rhs, inverse_blocks, update_blocks, asm_owner, asm_row):
    leaf_rows = SPLIT * PIV_DEV
    row_ids = jnp.arange(ROWS, dtype=jnp.int32)
    leaf_of = row_ids // leaf_rows
    targets = []
    for level_index in range(LEVELS - 1):
        owner_ids = asm_owner[level_index, :, 0]
        upper_side = owner_ids // SPLIT
        front_of = owner_ids % SPLIT
        pair_span = 2 ** level_index
        lower_leaf = leaf_of - (leaf_of // pair_span) % 2 * pair_span
        targets.append(((lower_leaf + upper_side * pair_span) * SPLIT + front_of) * PIV_DEV + asm_row[level_index])
    assembled = jnp.zeros((ROWS, RHS), jnp.float32)
    solved_all = []
    for level_index in range(LEVELS):
        front_rows = leaf_rows * 2 ** level_index
        column_start = leaf_rows * (2 ** level_index - 1)
        pivots = (rhs[level_index].astype(jnp.float32) - assembled).astype(jnp.bfloat16)
        solved = apply_blocks(inverse_blocks[:, column_start:column_start + front_rows], pivots, front_rows).astype(jnp.bfloat16)
        solved_all.append(solved)
        if level_index + 1 < LEVELS:
            update = apply_blocks(update_blocks[:, column_start:column_start + front_rows], solved, front_rows).astype(jnp.bfloat16)
            assembled = jnp.zeros((ROWS, RHS), jnp.float32).at[targets[level_index]].add(update.astype(jnp.float32))
    solutions = [None] * LEVELS
    below = None
    for level_index in reversed(range(LEVELS)):
        front_rows = leaf_rows * 2 ** level_index
        column_start = leaf_rows * (2 ** level_index - 1)
        if level_index + 1 == LEVELS:
            weights = solved_all[level_index]
        else:
            fetched = below[targets[level_index]]
            carried = apply_transposed(update_blocks[:, column_start:column_start + front_rows], fetched, front_rows)
            weights = (solved_all[level_index].astype(jnp.float32) - carried).astype(jnp.bfloat16)
        solution = apply_transposed(inverse_blocks[:, column_start:column_start + front_rows], weights, front_rows)
        solutions[level_index] = solution
        below = solution.astype(jnp.bfloat16)
    return jnp.stack(solutions)
```

```python
import jax
import jax.numpy as jnp
from jax import lax
from jax.sharding import PartitionSpec as P

LEVELS = 3
BF16 = jnp.bfloat16


def swapped(shard, axis, distance):
    return lax.ppermute(shard, axis, [(i, i ^ 1 << distance) for i in range(lax.axis_size(axis))])


def product(left, right, left_dim, right_dim):
    return lax.dot_general(
        left, right, (((left_dim,), (right_dim,)), ((), ())), preferred_element_type=jnp.float32
    )


def forward(vector, matrix):
    return product(vector, matrix, 1, 1)


def adjoint(vector, matrix):
    return product(vector, matrix, 1, 0)


def ordered(own, other, upper, axis):
    return jnp.where(
        upper == 1,
        jnp.concatenate([other, own], axis),
        jnp.concatenate([own, other], axis),
    )


def part(array, index, count, axis):
    size = array.shape[axis] // count
    return lax.dynamic_slice_in_dim(array, index * size, size, axis)


def shards(rhs, inverse_blocks, update_blocks, asm_owner, asm_row):
    own_rows, rhs_cols = rhs.shape[1:]
    front_count = lax.axis_size("front")
    leaf_rows = front_count * own_rows
    leaf_id = lax.axis_index("leaf")
    front_id = lax.axis_index("front")
    odd = front_id % 2
    side = leaf_id % 2
    wing = leaf_id // 2 % 2
    high_bits = range(1, front_count.bit_length() - 1)

    def high_gather(block, axis):
        for bit in high_bits:
            block = ordered(block, swapped(block, "front", bit), front_id >> bit & 1, axis)
        return block

    inverse0 = inverse_blocks[:, :leaf_rows]
    inverse1 = inverse_blocks[:, leaf_rows : 3 * leaf_rows]
    inverse2 = inverse_blocks[:, 3 * leaf_rows :]

    lists = jnp.concatenate([asm_owner[:, :, 0], asm_row], 0).astype(BF16)
    lists = jnp.pad(lists, ((0, 12), (0, 0)))
    kept = part(rhs, odd, 2, 2).reshape(LEVELS * own_rows, -1)
    handed = part(rhs, 1 - odd, 2, 2).reshape(LEVELS * own_rows, -1)
    lists_wide = jnp.pad(lists, ((0, 0), (0, kept.shape[1] - own_rows)))
    received = swapped(jnp.concatenate([handed, lists_wide], 0), "front", 0)
    kept = jnp.concatenate([kept, lists_wide], 0)
    inverse0_pair = swapped(inverse0, "front", 0)
    update_pair = swapped(update_blocks, "front", 0)
    inverse1_leaf = lax.all_gather(inverse1, "front", axis=0, tiled=True)

    def level_rows(level_index):
        return ordered(
            kept[level_index * own_rows : (level_index + 1) * own_rows],
            received[level_index * own_rows : (level_index + 1) * own_rows],
            odd,
            0,
        )

    rhs0 = high_gather(level_rows(0), 0)
    later = jnp.concatenate(
        [
            level_rows(1).T,
            level_rows(2).T,
            ordered(
                kept[LEVELS * own_rows :, :own_rows], received[LEVELS * own_rows :, :own_rows], odd, 1
            ),
        ],
        0,
    )
    later = high_gather(later, 1)
    half_cols = rhs_cols // 2
    rhs1 = later[:half_cols]
    rhs2 = later[half_cols : 2 * half_cols]
    lists = later[2 * half_cols : 2 * half_cols + 4].astype(jnp.int32)

    def selector(level_index):
        target = lists[level_index : level_index + 1] * own_rows + lists[2 + level_index : 3 + level_index]
        return (jnp.arange(2 * leaf_rows)[:, None] == target).astype(BF16)

    def placed_in(block, upper):
        zeros = jnp.zeros_like(block)
        return ordered(block, zeros, upper, 1)

    def pair_product(vector, own, other):
        return ordered(forward(vector, own), forward(vector, other), odd, 1).astype(BF16)

    solved0 = high_gather(
        ordered(
            product(rhs0, inverse0, 0, 1), product(rhs0, inverse0_pair, 0, 1), odd, 1
        ).astype(BF16),
        1,
    )
    update0 = high_gather(
        pair_product(solved0, update_blocks[:, :leaf_rows], update_pair[:, :leaf_rows]), 1
    )
    select0 = selector(0)
    pivots1 = placed_in(rhs1, side).astype(jnp.float32) - forward(update0, select0)
    pivots1 = (pivots1 + swapped(pivots1.astype(BF16), "leaf", 0).astype(jnp.float32)).astype(BF16)

    solved1 = forward(pivots1, inverse1_leaf).astype(BF16)
    solved1_all = ordered(solved1, swapped(solved1, "leaf", 0), side, 1)
    update1 = high_gather(
        pair_product(solved1_all, update_blocks[:, leaf_rows:], update_pair[:, leaf_rows:]), 1
    )
    select1 = selector(1)
    pivots2 = placed_in(rhs2, wing).astype(jnp.float32) - forward(update1, select1)
    pivots2 = (
        part(pivots2, wing, 2, 0)
        + swapped(part(pivots2, 1 - wing, 2, 0).astype(BF16), "leaf", 1).astype(jnp.float32)
    ).astype(BF16)
    pivots2 = ordered(
        pivots2.reshape(-1, 2, 1, leaf_rows),
        swapped(pivots2, "leaf", 0).reshape(-1, 2, 1, leaf_rows),
        side,
        2,
    ).reshape(-1, 4 * leaf_rows)

    inverse2_wing = swapped(inverse2, "leaf", 1)
    inverse2_all = jnp.concatenate(
        [inverse2, inverse2_wing, swapped(inverse2, "front", 0), swapped(inverse2_wing, "front", 0)], 0
    )
    solved2 = forward(pivots2, inverse2_all).astype(BF16)
    below2 = adjoint(solved2, inverse2_all).reshape(-1, 2, 2, leaf_rows)
    handed2 = lax.dynamic_index_in_dim(below2, 1 - side, 2, False).reshape(-1, 2 * leaf_rows)
    below2 = lax.dynamic_index_in_dim(below2, side, 2, False).reshape(-1, 2 * leaf_rows)
    below2 = below2 + swapped(handed2.astype(BF16), "leaf", 0).astype(jnp.float32)
    for bit in high_bits:
        below2 = below2 + swapped(below2.astype(BF16), "front", bit).astype(jnp.float32)
    below2 = below2.astype(BF16)
    below2 = ordered(below2, swapped(below2, "leaf", 1), wing, 0)

    update1_leaf = lax.all_gather(update_blocks[:, leaf_rows:], "front", axis=0, tiled=True)
    fetched1 = adjoint(below2, select1).astype(BF16)
    carried1 = adjoint(fetched1, update1_leaf)
    carried1 = part(carried1, side, 2, 1) + swapped(
        part(carried1, 1 - side, 2, 1).astype(BF16), "leaf", 0
    ).astype(jnp.float32)
    weights1 = (solved1.astype(jnp.float32) - carried1).astype(BF16)
    below1 = adjoint(weights1, inverse1_leaf)
    below1 = (below1 + swapped(below1.astype(BF16), "leaf", 0).astype(jnp.float32)).astype(BF16)

    level0_leaf = lax.all_gather(
        jnp.concatenate([inverse0, update_blocks[:, :leaf_rows]], 1), "front", axis=0, tiled=True
    )
    fetched0 = adjoint(below1, select0).astype(BF16)
    weights0 = solved0.astype(jnp.float32) - adjoint(fetched0, level0_leaf[:, leaf_rows:])
    below0 = adjoint(weights0.astype(BF16), level0_leaf[:, :leaf_rows])

    def own_columns(block):
        return part(block, front_id, front_count, 1), part(block, front_id ^ 1, front_count, 1)

    def finished(block):
        own, other = own_columns(block)
        other = swapped(other.astype(BF16), "front", 0).astype(jnp.float32)
        return ordered(own.astype(jnp.float32), other, odd, 0).T

    return jnp.stack(
        [finished(below0), finished(part(below1, side, 2, 1)), finished(part(below2, wing, 2, 1))]
    )


def solution(mesh):
    placed = (
        P(None, ("leaf", "front"), None),
        P(("leaf", "front"), None),
        P(("leaf", "front"), None),
        P(None, ("leaf", "front"), None),
        P(None, ("leaf", "front")),
    )
    return jax.shard_map(
        shards,
        mesh=mesh,
        in_specs=placed,
        out_specs=P(None, ("leaf", "front"), None),
        check_vma=False,
    )
```

```python
import jax
import jax.numpy as jnp
from jax import lax
from jax.sharding import PartitionSpec as P

LEVELS = 3
BF16 = jnp.bfloat16
F32 = jnp.float32


def swapped(shard, axis, distance):
    return lax.ppermute(shard, axis, [(i, i ^ 1 << distance) for i in range(lax.axis_size(axis))])


def product(left, right, left_dim, right_dim):
    return lax.dot_general(
        left, right, (((left_dim,), (right_dim,)), ((), ())), preferred_element_type=F32
    )


def forward(vector, matrix):
    return product(vector, matrix, 1, 1)


def adjoint(vector, matrix):
    return product(vector, matrix, 1, 0)


def ordered(own, other, upper, axis):
    return jnp.where(
        upper == 1,
        jnp.concatenate([other, own], axis),
        jnp.concatenate([own, other], axis),
    )


def after(array, *earlier):
    return lax.optimization_barrier((array, *earlier))[0]


def together(*arrays):
    return lax.optimization_barrier(arrays)


def part(array, index, count, axis):
    size = array.shape[axis] // count
    return lax.dynamic_slice_in_dim(array, index * size, size, axis)


def shards(rhs, inverse_blocks, update_blocks, asm_owner, asm_row):
    own_rows, rhs_cols = rhs.shape[1:]
    front_count = lax.axis_size("front")
    leaf_rows = front_count * own_rows
    half_cols = rhs_cols // 2
    leaf_id = lax.axis_index("leaf")
    front_id = lax.axis_index("front")
    odd = front_id % 2
    side = leaf_id % 2
    wing = leaf_id // 2 % 2
    high_bits = range(1, front_count.bit_length() - 1)

    def high_gather(block, axis):
        for bit in high_bits:
            block = ordered(block, swapped(block, "front", bit), front_id >> bit & 1, axis)
        return block

    def high_scatter(block):
        for bit in reversed(high_bits):
            upper = front_id >> bit & 1
            block = part(block, upper, 2, 1) + swapped(
                part(block, 1 - upper, 2, 1).astype(BF16), "front", bit
            ).astype(F32)
        return block

    def high_sum(block):
        for bit in high_bits:
            block = block + swapped(block.astype(BF16), "front", bit).astype(F32)
        return block

    def side_scatter(block):
        return part(block, side, 2, 1) + swapped(
            part(block, 1 - side, 2, 1).astype(BF16), "leaf", 0
        ).astype(F32)

    def pair_rows(block):
        return part(block, front_id // 2, front_count // 2, 1)

    def pair_forward(vector, own, other):
        return ordered(forward(vector, own), forward(vector, other), odd, 1).astype(BF16)

    def pair_adjoint(vector, own, other):
        return adjoint(part(vector, odd, 2, 1), own) + adjoint(part(vector, 1 - odd, 2, 1), other)

    inverse0 = inverse_blocks[:, :leaf_rows]
    inverse1 = inverse_blocks[:, leaf_rows : 3 * leaf_rows]
    inverse2 = inverse_blocks[:, 3 * leaf_rows :]
    update0 = update_blocks[:, :leaf_rows]
    update1 = update_blocks[:, leaf_rows:]

    rhs0 = ordered(
        part(rhs[0], odd, 2, 1), swapped(part(rhs[0], 1 - odd, 2, 1), "front", 0), odd, 0
    )
    inverse0_pair = swapped(inverse0, "front", 0)
    update0_pair = swapped(after(update0, rhs0), "front", 0)
    wing2 = swapped(after(inverse2, rhs0), "leaf", 1)

    lists = jnp.concatenate([asm_owner[:, :, 0], asm_row], 0).astype(BF16)
    lists = jnp.pad(lists, ((0, 12), (0, half_cols - own_rows)))
    kept = jnp.concatenate([part(rhs[1:], odd, 2, 2).reshape(2 * own_rows, -1), lists], 0)
    handed = jnp.concatenate([part(rhs[1:], 1 - odd, 2, 2).reshape(2 * own_rows, -1), lists], 0)
    received = swapped(after(handed, rhs0), "front", 0)

    rhs0_leaf = high_gather(rhs0, 0)
    rhs0_leaf, inverse0_pair, received = together(rhs0_leaf, inverse0_pair, received)
    solved0_pair = ordered(
        product(rhs0_leaf, inverse0, 0, 1), product(rhs0_leaf, inverse0_pair, 0, 1), odd, 1
    ).astype(BF16)
    inverse1_pair = swapped(after(inverse1, solved0_pair), "front", 0)
    solved0 = high_gather(solved0_pair, 1)
    solved0, update0_pair, inverse1_pair = together(solved0, update0_pair, inverse1_pair)

    def level_rows(index):
        rows = slice(index * own_rows, (index + 1) * own_rows)
        return ordered(kept[rows], received[rows], odd, 0).T

    lists = ordered(
        kept[2 * own_rows :, :own_rows], received[2 * own_rows :, :own_rows], odd, 1
    )
    rhs1 = level_rows(0)
    rhs2 = level_rows(1)
    updated0_pair = pair_forward(solved0, update0, update0_pair)
    update1_pair = swapped(after(update1, updated0_pair), "front", 0)
    updated0 = high_gather(jnp.concatenate([updated0_pair, rhs1, lists], 0), 1)
    updated0, wing2 = together(updated0, wing2)
    lists = updated0[2 * half_cols : 2 * half_cols + 4].astype(jnp.int32)
    rhs1 = updated0[half_cols : 2 * half_cols]
    updated0 = updated0[:half_cols]

    def selector(level_index):
        target = lists[level_index : level_index + 1] * own_rows + lists[2 + level_index : 3 + level_index]
        return (jnp.arange(2 * leaf_rows)[:, None] == target).astype(BF16)

    select0 = selector(0)
    select1 = selector(1)
    pivots1 = ordered(rhs1, jnp.zeros_like(rhs1), side, 1).astype(F32) - forward(updated0, select0)
    pivots1 = (pivots1 + swapped(pivots1.astype(BF16), "leaf", 0).astype(F32)).astype(BF16)

    solved1_pair = pair_forward(pivots1, inverse1, inverse1_pair)
    solved1 = high_gather(solved1_pair, 1)
    solved1, update1_pair = together(solved1, update1_pair)
    solved1 = ordered(solved1, swapped(solved1, "leaf", 0), side, 1)
    updated1_pair = pair_forward(solved1, update1, update1_pair)
    updated1 = high_gather(jnp.concatenate([updated1_pair, rhs2], 0), 1)
    rhs2 = updated1[half_cols:]
    updated1 = updated1[:half_cols]

    def stacked(block):
        return jnp.concatenate([block[:, :leaf_rows], block[:, leaf_rows:]], 0)

    def flat(block):
        cols = block.shape[0] // 2
        return block[:cols], block[cols:]

    pivots2 = ordered(rhs2, jnp.zeros_like(rhs2), wing, 1).astype(F32) - forward(updated1, select1)
    pivots2 = (
        stacked(part(pivots2, wing, 2, 0))
        + swapped(stacked(part(pivots2, 1 - wing, 2, 0)).astype(BF16), "leaf", 1).astype(F32)
    ).astype(BF16)
    pivots2 = jnp.concatenate(
        [
            jnp.concatenate(pieces, 0)
            for pieces in zip(flat(pivots2), flat(swapped(pivots2, "front", 0)))
        ],
        0,
    )
    other2 = swapped(pivots2, "leaf", 0)
    low2 = flat(jnp.where(side == 1, other2, pivots2))
    high2 = flat(jnp.where(side == 1, pivots2, other2))
    pivots2 = jnp.concatenate([low2[0], high2[0], low2[1], high2[1]], 1)
    inverse2_all = jnp.concatenate([inverse2, wing2], 0)
    solved2 = forward(pivots2, inverse2_all).astype(BF16)
    below2 = adjoint(solved2, inverse2_all)
    leaves = [below2[:, i * leaf_rows : (i + 1) * leaf_rows] for i in range(4)]
    low2 = jnp.concatenate([leaves[0], leaves[2]], 0)
    high2 = jnp.concatenate([leaves[1], leaves[3]], 0)
    handed2 = jnp.where(side == 1, low2, high2).astype(BF16)
    below2 = jnp.where(side == 1, high2, low2) + swapped(handed2, "leaf", 0).astype(F32)
    quarter = half_cols // 2
    low2, high2 = flat(below2)
    handed2 = jnp.concatenate([low2[quarter:], high2[quarter:]], 0).astype(BF16)
    below2 = jnp.concatenate([low2[:quarter], high2[:quarter]], 0)
    below2 = below2 + swapped(handed2, "front", 0).astype(F32)
    below2 = high_sum(below2).astype(BF16)
    own2 = flat(below2)
    other2 = flat(swapped(below2, "leaf", 1))
    below2 = jnp.concatenate(
        [ordered(own, other, wing, 0) for own, other in zip(own2, other2)], 1
    )

    fetched1 = adjoint(below2, pair_rows(select1)).astype(BF16)
    carried1 = pair_adjoint(fetched1, update1, update1_pair)
    weights1 = (solved1_pair.astype(F32) - high_scatter(side_scatter(carried1))).astype(BF16)
    below1 = high_sum(side_scatter(pair_adjoint(weights1, inverse1, inverse1_pair))).astype(BF16)
    below1_all = ordered(below1, swapped(below1, "leaf", 0), side, 1)

    fetched0 = adjoint(below1_all, pair_rows(select0)).astype(BF16)
    carried0 = pair_adjoint(fetched0, update0, update0_pair)
    weights0 = (solved0_pair.astype(F32) - high_scatter(carried0)).astype(BF16)
    below0 = high_scatter(pair_adjoint(weights0, inverse0, inverse0_pair))

    def finished(block):
        other = swapped(part(block, 1 - odd, 2, 1).astype(BF16), "front", 0).astype(F32)
        return ordered(part(block, odd, 2, 1).astype(F32), other, odd, 0).T

    return jnp.stack(
        [
            finished(below0),
            finished(pair_rows(below1)),
            finished(pair_rows(part(below2, wing, 2, 1))),
        ]
    )


def solution(mesh):
    placed = (
        P(None, ("leaf", "front"), None),
        P(("leaf", "front"), None),
        P(("leaf", "front"), None),
        P(None, ("leaf", "front"), None),
        P(None, ("leaf", "front")),
    )
    return jax.shard_map(
        shards,
        mesh=mesh,
        in_specs=placed,
        out_specs=P(None, ("leaf", "front"), None),
        check_vma=False,
    )
```

```python
import jax
import jax.numpy as jnp
from jax import lax
from jax.sharding import PartitionSpec as P

LEVELS = 3
BF16 = jnp.bfloat16
F32 = jnp.float32


def traded(shard, axis, mask):
    return lax.ppermute(shard, axis, [(i, i ^ mask) for i in range(lax.axis_size(axis))])


def product(left, right, left_dim, right_dim):
    return lax.dot_general(
        left, right, (((left_dim,), (right_dim,)), ((), ())), preferred_element_type=F32
    )


def forward(vector, matrix):
    return product(vector, matrix, 1, 1)


def adjoint(vector, matrix):
    return product(vector, matrix, 1, 0)


def ordered(own, other, upper, axis):
    return jnp.where(
        upper == 1,
        jnp.concatenate([other, own], axis),
        jnp.concatenate([own, other], axis),
    )


def after(array, *earlier):
    return lax.optimization_barrier((array, *earlier))[0]


def together(*arrays):
    return lax.optimization_barrier(arrays)


def part(array, index, count, axis):
    size = array.shape[axis] // count
    return lax.dynamic_slice_in_dim(array, index * size, size, axis)


def stacked(block):
    middle = block.shape[1] // 2
    return jnp.concatenate([block[:, :middle], block[:, middle:]], 0)


def flat(block):
    middle = block.shape[0] // 2
    return block[:middle], block[middle:]


def shards(rhs, inverse_blocks, update_blocks, asm_owner, asm_row):
    own_rows, rhs_cols = rhs.shape[1:]
    front_count = lax.axis_size("front")
    leaf_rows = front_count * own_rows
    half_cols = rhs_cols // 2
    quarter = half_cols // 2
    leaf_id = lax.axis_index("leaf")
    front_id = lax.axis_index("front")
    odd = front_id % 2
    side = leaf_id % 2
    wing = leaf_id // 2 % 2
    high_bits = range(1, front_count.bit_length() - 1)

    def high_gather(*blocks):
        for bit in high_bits:
            received = traded(jnp.concatenate(blocks, 1), "front", 1 << bit)
            ends = [sum(b.shape[1] for b in blocks[: i + 1]) for i in range(len(blocks))]
            blocks = [
                ordered(b, received[:, end - b.shape[1] : end], front_id >> bit & 1, 1)
                for b, end in zip(blocks, ends)
            ]
        return blocks[0] if len(blocks) == 1 else blocks

    def high_scatter(block):
        for bit in reversed(high_bits):
            upper = front_id >> bit & 1
            block = part(block, upper, 2, 1).astype(F32) + traded(
                part(block, 1 - upper, 2, 1).astype(BF16), "front", 1 << bit
            ).astype(F32)
        return block

    def side_scatter(block):
        return part(block, side, 2, 1) + traded(
            part(block, 1 - side, 2, 1).astype(BF16), "leaf", 1
        ).astype(F32)

    def pair_forward(vector, own, other):
        return ordered(forward(vector, own), forward(vector, other), odd, 1).astype(BF16)

    def pair_adjoint(vector, own, other):
        return adjoint(part(vector, odd, 2, 1), own) + adjoint(part(vector, 1 - odd, 2, 1), other)

    def high_sum(block):
        for bit in high_bits:
            block = block + traded(block.astype(BF16), "front", 1 << bit).astype(F32)
        return block

    def pair_rows(block):
        return part(block, front_id // 2, front_count // 2, 1)

    def high_pieces(own):
        pieces = [own]
        for bit in high_bits:
            pieces += [traded(piece, "front", 1 << bit) for piece in pieces]
        return pieces

    def in_order(blocks, axis):
        for bit in range(front_count.bit_length() - 1):
            blocks = [
                ordered(blocks[i], blocks[i + 1], front_id >> bit & 1, axis)
                for i in range(0, len(blocks), 2)
            ]
        return blocks[0]

    def leaf_forward(vector, pieces):
        return in_order([forward(vector, piece) for piece in pieces], 1).astype(BF16)

    def leaf_adjoint(vector, pieces):
        return sum(
            adjoint(part(vector, front_id ^ i, front_count, 1), piece)
            for i, piece in enumerate(pieces)
        )

    def alternated(even, odd_ones):
        return [piece for pieces in zip(even, odd_ones) for piece in pieces]

    inverse0 = inverse_blocks[:, :leaf_rows]
    inverse1 = inverse_blocks[:, leaf_rows : 3 * leaf_rows]
    inverse2 = inverse_blocks[:, 3 * leaf_rows :]
    update0 = update_blocks[:, :leaf_rows]
    update1 = update_blocks[:, leaf_rows:]
    inverse0 = lax.optimization_barrier(inverse0)
    inverse1 = lax.optimization_barrier(inverse1)
    inverse2 = lax.optimization_barrier(inverse2)
    update0 = lax.optimization_barrier(update0)
    update1 = lax.optimization_barrier(update1)

    first = jnp.concatenate([inverse0, rhs[0]], 1)
    first_even = high_pieces(first)
    inverse0_near = traded(inverse0, "front", 1)
    count = len(first_even)

    lists = jnp.concatenate([asm_owner[:, :, 0], asm_row], 0).astype(BF16)
    kept = part(rhs[1:], odd, 2, 2).reshape(2 * own_rows, -1)
    handed = part(rhs[1:], 1 - odd, 2, 2).reshape(2 * own_rows, -1)
    received = traded(
        after(jnp.concatenate([handed, lists.reshape(-1, half_cols)], 0), first), "front", 1
    )


    def level_rows(index):
        rows = slice(index * own_rows, (index + 1) * own_rows)
        return ordered(kept[rows], received[rows], odd, 0).T

    def as_block(lists):
        return lists.reshape(-1, half_cols).T

    lists = ordered(lists, received[2 * own_rows :].reshape(4, -1), odd, 1)
    rhs1, rhs2, *lists = high_gather(
        level_rows(0), level_rows(1), *(as_block(lists[i : i + 1]) for i in range(4))
    )
    lists = jnp.concatenate([block.T.reshape(1, -1) for block in lists], 0)

    through = traded(
        jnp.concatenate(
            [part(block[:, leaf_rows:], 1 - odd, 2, 1) for block in first_even]
            + [block[:, :leaf_rows] for block in first_even[1:]],
            1,
        ),
        "front",
        1,
    )
    update0_pair = traded(after(update0, first_even[-1]), "front", 1)
    wing2 = traded(after(inverse2, first), "leaf", 2)
    through, inverse0_near, update0_pair = together(through, inverse0_near, update0_pair)
    rhs0_leaf = in_order(
        alternated(
            [part(block[:, leaf_rows:], odd, 2, 1) for block in first_even],
            [through[:, i * half_cols : (i + 1) * half_cols] for i in range(count)],
        ),
        0,
    )
    inverse0_pieces = alternated(
        [block[:, :leaf_rows] for block in first_even],
        [inverse0_near]
        + [through[:, count * half_cols + i * leaf_rows :][:, :leaf_rows] for i in range(count - 1)],
    )

    solved0 = in_order([product(rhs0_leaf, piece, 0, 1) for piece in inverse0_pieces], 1).astype(BF16)
    updated0_pair = pair_forward(solved0, update0, update0_pair)
    inverse1_pair = traded(after(inverse1, solved0), "front", 1)
    updated0 = high_gather(updated0_pair)
    updated0, inverse1_pair, rhs1, rhs2, lists, wing2 = together(
        updated0, inverse1_pair, rhs1, rhs2, lists, wing2
    )
    update1_pair = traded(after(update1, updated0), "front", 1)

    def selector(level_index):
        numbers = lists.astype(jnp.int32)
        target = numbers[level_index : level_index + 1] * own_rows + numbers[2 + level_index : 3 + level_index]
        return (jnp.arange(2 * leaf_rows)[:, None] == target).astype(BF16)

    select0 = selector(0)
    select1 = selector(1)
    pivots1 = ordered(rhs1, jnp.zeros_like(rhs1), side, 1).astype(F32) - forward(updated0, select0)
    pivots1 = (pivots1 + traded(pivots1.astype(BF16), "leaf", 1).astype(F32)).astype(BF16)

    solved1_pair = pair_forward(pivots1, inverse1, inverse1_pair)
    solved0_late, update0_late = together(solved0, update0, solved1_pair)[:2]
    straight0 = pair_rows(leaf_adjoint(solved0_late, inverse0_pieces))
    both0 = leaf_adjoint(update0_late, inverse0_pieces).astype(BF16)
    both0_pair = leaf_adjoint(update0_pair, inverse0_pieces).astype(BF16)
    solved1 = high_gather(solved1_pair)
    solved1, straight0, both0, both0_pair, update1_pair = together(solved1, straight0, both0, both0_pair, update1_pair)
    solved1 = ordered(solved1, traded(solved1, "leaf", 1), side, 1)
    updated1_pair = pair_forward(solved1, update1, update1_pair)
    updated1 = high_gather(updated1_pair)

    pivots2 = ordered(rhs2, jnp.zeros_like(rhs2), wing, 1).astype(F32) - forward(updated1, select1)
    pivots2 = (
        stacked(part(pivots2, wing, 2, 0))
        + traded(stacked(part(pivots2, 1 - wing, 2, 0)).astype(BF16), "leaf", 2).astype(F32)
    ).astype(BF16)
    pivots2 = jnp.concatenate(
        [
            jnp.concatenate(pieces, 0)
            for pieces in zip(flat(pivots2), flat(traded(pivots2, "front", 1)))
        ],
        0,
    )
    other2 = traded(pivots2, "leaf", 1)
    low2 = flat(jnp.where(side == 1, other2, pivots2))
    high2 = flat(jnp.where(side == 1, pivots2, other2))
    pivots2 = jnp.concatenate([low2[0], high2[0], low2[1], high2[1]], 1)
    below2 = adjoint(forward(pivots2, inverse2).astype(BF16), inverse2) + adjoint(
        forward(pivots2, wing2).astype(BF16), wing2
    )
    leaves = [below2[:, i * leaf_rows : (i + 1) * leaf_rows] for i in range(4)]
    low2 = jnp.concatenate([leaves[0], leaves[2]], 0)
    high2 = jnp.concatenate([leaves[1], leaves[3]], 0)
    handed2 = jnp.where(side == 1, low2, high2).astype(BF16)
    below2 = jnp.where(side == 1, high2, low2) + traded(handed2, "leaf", 1).astype(F32)
    low2, high2 = flat(below2)
    handed2 = jnp.concatenate([low2[quarter:], high2[quarter:]], 0).astype(BF16)
    below2 = jnp.concatenate([low2[:quarter], high2[:quarter]], 0)
    below2 = below2 + traded(handed2, "front", 1).astype(F32)
    below2 = high_sum(below2).astype(BF16)
    own2 = flat(below2)
    other2 = flat(traded(below2, "leaf", 2))
    below2 = jnp.concatenate(
        [ordered(own, other, wing, 0) for own, other in zip(own2, other2)], 1
    )

    fetched1 = adjoint(below2, pair_rows(select1)).astype(BF16)
    carried1 = pair_adjoint(fetched1, update1, update1_pair)
    weights1 = (solved1_pair.astype(F32) - high_scatter(side_scatter(carried1))).astype(BF16)
    below1 = high_sum(side_scatter(pair_adjoint(weights1, inverse1, inverse1_pair))).astype(BF16)
    below1_all = ordered(below1, traded(below1, "leaf", 1), side, 1)

    fetched0 = adjoint(below1_all, pair_rows(select0)).astype(BF16)
    carried0 = pair_adjoint(fetched0, both0, both0_pair)
    upper = jnp.concatenate([pair_rows(below1), pair_rows(part(below2, wing, 2, 1))], 0)
    upper, carried0 = together(upper, carried0)
    upper_other = traded(part(upper, 1 - odd, 2, 1), "front", 1)
    carried0, upper_other = together(high_scatter(carried0), upper_other)
    below0 = straight0 - carried0
    below0_other = traded(part(below0, 1 - odd, 2, 1).astype(BF16), "front", 1)

    def finished(own, other):
        return ordered(own.astype(F32), other.astype(F32), odd, 0).T

    upper = part(upper, odd, 2, 1)
    return jnp.stack(
        [
            finished(part(below0, odd, 2, 1), below0_other),
            finished(upper[:half_cols], upper_other[:half_cols]),
            finished(upper[half_cols:], upper_other[half_cols:]),
        ]
    )


def solution(mesh):
    placed = (
        P(None, ("leaf", "front"), None),
        P(("leaf", "front"), None),
        P(("leaf", "front"), None),
        P(None, ("leaf", "front"), None),
        P(None, ("leaf", "front")),
    )
    return jax.shard_map(
        shards,
        mesh=mesh,
        in_specs=placed,
        out_specs=P(None, ("leaf", "front"), None),
        check_vma=False,
    )
```

```python
import jax
import jax.numpy as jnp
from jax import lax
from jax.sharding import PartitionSpec as P

LEVELS = 3
BF16 = jnp.bfloat16
F32 = jnp.float32


def traded(shard, axis, mask):
    return lax.ppermute(shard, axis, [(i, i ^ mask) for i in range(lax.axis_size(axis))])


def product(left, right, left_dim, right_dim):
    return lax.dot_general(
        left, right, (((left_dim,), (right_dim,)), ((), ())), preferred_element_type=F32
    )


def forward(vector, matrix):
    return product(vector, matrix, 1, 1)


def adjoint(vector, matrix):
    return product(vector, matrix, 1, 0)


def ordered(own, other, upper, axis):
    return jnp.where(
        upper == 1,
        jnp.concatenate([other, own], axis),
        jnp.concatenate([own, other], axis),
    )


def after(array, *earlier):
    return lax.optimization_barrier((array, *earlier))[0]


def together(*arrays):
    return lax.optimization_barrier(arrays)


def part(array, index, count, axis):
    size = array.shape[axis] // count
    return lax.dynamic_slice_in_dim(array, index * size, size, axis)


def stacked(block):
    middle = block.shape[1] // 2
    return jnp.concatenate([block[:, :middle], block[:, middle:]], 0)


def flat(block):
    middle = block.shape[0] // 2
    return block[:middle], block[middle:]


def shards(rhs, inverse_blocks, update_blocks, asm_owner, asm_row):
    own_rows, rhs_cols = rhs.shape[1:]
    front_count = lax.axis_size("front")
    leaf_rows = front_count * own_rows
    half_cols = rhs_cols // 2
    quarter = half_cols // 2
    leaf_id = lax.axis_index("leaf")
    front_id = lax.axis_index("front")
    odd = front_id % 2
    side = leaf_id % 2
    wing = leaf_id // 2 % 2
    high_bits = range(1, front_count.bit_length() - 1)

    def high_gather(*blocks):
        for bit in high_bits:
            received = traded(jnp.concatenate(blocks, 1), "front", 1 << bit)
            ends = [sum(b.shape[1] for b in blocks[: i + 1]) for i in range(len(blocks))]
            blocks = [
                ordered(b, received[:, end - b.shape[1] : end], front_id >> bit & 1, 1)
                for b, end in zip(blocks, ends)
            ]
        return blocks[0] if len(blocks) == 1 else blocks

    def high_scatter(block):
        for bit in reversed(high_bits):
            upper = front_id >> bit & 1
            block = part(block, upper, 2, 1).astype(F32) + traded(
                part(block, 1 - upper, 2, 1).astype(BF16), "front", 1 << bit
            ).astype(F32)
        return block

    def side_scatter(block):
        return part(block, side, 2, 1) + traded(
            part(block, 1 - side, 2, 1).astype(BF16), "leaf", 1
        ).astype(F32)

    def pair_forward(vector, own, other):
        return ordered(forward(vector, own), forward(vector, other), odd, 1).astype(BF16)

    def pair_adjoint(vector, own, other):
        return adjoint(part(vector, odd, 2, 1), own) + adjoint(part(vector, 1 - odd, 2, 1), other)

    def high_sum(block):
        for bit in high_bits:
            block = block + traded(block.astype(BF16), "front", 1 << bit).astype(F32)
        return block

    def pair_rows(block):
        return part(block, front_id // 2, front_count // 2, 1)

    def high_pieces(own):
        pieces = [own]
        for bit in high_bits:
            pieces += [traded(piece, "front", 1 << bit) for piece in pieces]
        return pieces

    def in_order(blocks, axis):
        for bit in range(front_count.bit_length() - 1):
            blocks = [
                ordered(blocks[i], blocks[i + 1], front_id >> bit & 1, axis)
                for i in range(0, len(blocks), 2)
            ]
        return blocks[0]

    def leaf_forward(vector, pieces):
        return in_order([forward(vector, piece) for piece in pieces], 1).astype(BF16)

    def leaf_adjoint(vector, pieces):
        return sum(
            adjoint(part(vector, front_id ^ i, front_count, 1), piece)
            for i, piece in enumerate(pieces)
        )

    def alternated(even, odd_ones):
        return [piece for pieces in zip(even, odd_ones) for piece in pieces]

    inverse0 = inverse_blocks[:, :leaf_rows]
    inverse1 = inverse_blocks[:, leaf_rows : 3 * leaf_rows]
    inverse2 = inverse_blocks[:, 3 * leaf_rows :]
    update0 = update_blocks[:, :leaf_rows]
    update1 = update_blocks[:, leaf_rows:]
    inverse0 = lax.optimization_barrier(inverse0)
    inverse1 = lax.optimization_barrier(inverse1)
    inverse2 = lax.optimization_barrier(inverse2)
    update0 = lax.optimization_barrier(update0)
    update1 = lax.optimization_barrier(update1)

    lists = jnp.concatenate([asm_owner[:, :, 0], asm_row], 0).astype(BF16)
    lists = jnp.pad(lists, ((0, 4), (0, leaf_rows + LEVELS * half_cols - own_rows)))

    def parcel(half):
        columns = [part(rhs[level], half, 2, 1) for level in range(LEVELS)]
        return jnp.concatenate([jnp.concatenate([inverse0, *columns], 1), lists], 0)

    kept, handed = parcel(odd), parcel(1 - odd)
    parcels = [kept] + [
        traded(handed if mask % 2 else kept, "front", mask) for mask in range(1, front_count)
    ]
    update0_pair = traded(after(update0, handed), "front", 1)
    inverse1_pair = traded(after(inverse1, handed), "front", 1)
    *parcels, update0_pair = together(*parcels, update0_pair)
    inverse0_pieces = [block[:own_rows, :leaf_rows] for block in parcels]
    rhs0, rhs1, rhs2 = (
        in_order(
            [
                block[:own_rows, leaf_rows + level * half_cols : leaf_rows + (level + 1) * half_cols]
                for block in parcels
            ],
            0,
        )
        for level in range(LEVELS)
    )
    rhs1, rhs2 = rhs1.T, rhs2.T
    lists = in_order([block[own_rows : own_rows + 4, :own_rows] for block in parcels], 1)

    solved0 = in_order([product(rhs0, piece, 0, 1) for piece in inverse0_pieces], 1).astype(BF16)
    updated0_pair = pair_forward(solved0, update0, update0_pair)
    update1_pair = traded(after(update1, solved0), "front", 1)
    updated0 = high_gather(updated0_pair)
    updated0, inverse1_pair = together(updated0, inverse1_pair)
    wing2 = traded(after(inverse2, solved0), "leaf", 2)

    def selector(level_index):
        numbers = lists.astype(jnp.int32)
        target = numbers[level_index : level_index + 1] * own_rows + numbers[2 + level_index : 3 + level_index]
        return (jnp.arange(2 * leaf_rows)[:, None] == target).astype(BF16)

    select0 = selector(0)
    select1 = selector(1)
    pivots1 = ordered(rhs1, jnp.zeros_like(rhs1), side, 1).astype(F32) - forward(updated0, select0)
    pivots1 = (pivots1 + traded(pivots1.astype(BF16), "leaf", 1).astype(F32)).astype(BF16)

    solved1_pair = pair_forward(pivots1, inverse1, inverse1_pair)
    solved0_late, update0_late = together(solved0, update0, solved1_pair)[:2]
    straight0 = pair_rows(leaf_adjoint(solved0_late, inverse0_pieces))
    both0 = leaf_adjoint(update0_late, inverse0_pieces).astype(BF16)
    both0_pair = leaf_adjoint(update0_pair, inverse0_pieces).astype(BF16)
    solved1 = high_gather(solved1_pair)
    solved1, straight0, both0, both0_pair, update1_pair, wing2 = together(
        solved1, straight0, both0, both0_pair, update1_pair, wing2
    )
    solved1 = ordered(solved1, traded(solved1, "leaf", 1), side, 1)
    updated1_pair = pair_forward(solved1, update1, update1_pair)
    updated1 = high_gather(updated1_pair)

    pivots2 = ordered(rhs2, jnp.zeros_like(rhs2), wing, 1).astype(F32) - forward(updated1, select1)
    pivots2 = (
        stacked(part(pivots2, wing, 2, 0))
        + traded(stacked(part(pivots2, 1 - wing, 2, 0)).astype(BF16), "leaf", 2).astype(F32)
    ).astype(BF16)
    pivots2 = jnp.concatenate(
        [
            jnp.concatenate(pieces, 0)
            for pieces in zip(flat(pivots2), flat(traded(pivots2, "front", 1)))
        ],
        0,
    )
    other2 = traded(pivots2, "leaf", 1)
    low2 = flat(jnp.where(side == 1, other2, pivots2))
    high2 = flat(jnp.where(side == 1, pivots2, other2))
    pivots2 = jnp.concatenate([low2[0], high2[0], low2[1], high2[1]], 1)
    below2 = adjoint(forward(pivots2, inverse2).astype(BF16), inverse2) + adjoint(
        forward(pivots2, wing2).astype(BF16), wing2
    )
    leaves = [below2[:, i * leaf_rows : (i + 1) * leaf_rows] for i in range(4)]
    low2 = jnp.concatenate([leaves[0], leaves[2]], 0)
    high2 = jnp.concatenate([leaves[1], leaves[3]], 0)
    handed2 = jnp.where(side == 1, low2, high2).astype(BF16)
    below2 = jnp.where(side == 1, high2, low2) + traded(handed2, "leaf", 1).astype(F32)
    low2, high2 = flat(below2)
    handed2 = jnp.concatenate([low2[quarter:], high2[quarter:]], 0).astype(BF16)
    below2 = jnp.concatenate([low2[:quarter], high2[:quarter]], 0)
    below2 = below2 + traded(handed2, "front", 1).astype(F32)
    below2 = high_sum(below2).astype(BF16)
    own2 = flat(below2)
    other2 = flat(traded(below2, "leaf", 2))
    below2 = jnp.concatenate(
        [ordered(own, other, wing, 0) for own, other in zip(own2, other2)], 1
    )

    fetched1 = adjoint(below2, pair_rows(select1)).astype(BF16)
    carried1 = pair_adjoint(fetched1, update1, update1_pair)
    weights1 = (solved1_pair.astype(F32) - high_scatter(side_scatter(carried1))).astype(BF16)
    below1 = high_sum(side_scatter(pair_adjoint(weights1, inverse1, inverse1_pair))).astype(BF16)
    below1_all = ordered(below1, traded(below1, "leaf", 1), side, 1)

    fetched0 = adjoint(below1_all, pair_rows(select0)).astype(BF16)
    carried0 = pair_adjoint(fetched0, both0, both0_pair)
    upper = jnp.concatenate([pair_rows(below1), pair_rows(part(below2, wing, 2, 1))], 0)
    upper, carried0 = together(upper, carried0)
    upper_other = traded(part(upper, 1 - odd, 2, 1), "front", 1)
    carried0, upper_other = together(high_scatter(carried0), upper_other)
    below0 = straight0 - carried0
    below0_other = traded(part(below0, 1 - odd, 2, 1).astype(BF16), "front", 1)

    def finished(own, other):
        return ordered(own.astype(F32), other.astype(F32), odd, 0).T

    upper = part(upper, odd, 2, 1)
    return jnp.stack(
        [
            finished(part(below0, odd, 2, 1), below0_other),
            finished(upper[:half_cols], upper_other[:half_cols]),
            finished(upper[half_cols:], upper_other[half_cols:]),
        ]
    )


def solution(mesh):
    placed = (
        P(None, ("leaf", "front"), None),
        P(("leaf", "front"), None),
        P(("leaf", "front"), None),
        P(None, ("leaf", "front"), None),
        P(None, ("leaf", "front")),
    )
    return jax.shard_map(
        shards,
        mesh=mesh,
        in_specs=placed,
        out_specs=P(None, ("leaf", "front"), None),
        check_vma=False,
    )
```

```python
import jax
import jax.numpy as jnp
from jax import lax
from jax.sharding import PartitionSpec as P

LEVELS = 3
BF16 = jnp.bfloat16
F32 = jnp.float32


def traded(shard, axis, mask):
    return lax.ppermute(shard, axis, [(i, i ^ mask) for i in range(lax.axis_size(axis))])


def product(left, right, left_dim, right_dim):
    return lax.dot_general(
        left, right, (((left_dim,), (right_dim,)), ((), ())), preferred_element_type=F32
    )


def forward(vector, matrix):
    return product(vector, matrix, 1, 1)


def adjoint(vector, matrix):
    return product(vector, matrix, 1, 0)


def ordered(own, other, upper, axis):
    return jnp.where(
        upper == 1,
        jnp.concatenate([other, own], axis),
        jnp.concatenate([own, other], axis),
    )


def after(array, *earlier):
    return lax.optimization_barrier((array, *earlier))[0]


def together(*arrays):
    return lax.optimization_barrier(arrays)


def part(array, index, count, axis):
    size = array.shape[axis] // count
    return lax.dynamic_slice_in_dim(array, index * size, size, axis)


def stacked(block):
    middle = block.shape[1] // 2
    return jnp.concatenate([block[:, :middle], block[:, middle:]], 0)


def flat(block):
    middle = block.shape[0] // 2
    return block[:middle], block[middle:]


def shards(rhs, inverse_blocks, update_blocks, asm_owner, asm_row):
    own_rows, rhs_cols = rhs.shape[1:]
    front_count = lax.axis_size("front")
    leaf_rows = front_count * own_rows
    half_cols = rhs_cols // 2
    quarter = half_cols // 2
    leaf_id = lax.axis_index("leaf")
    front_id = lax.axis_index("front")
    odd = front_id % 2
    side = leaf_id % 2
    wing = leaf_id // 2 % 2
    high_bits = range(1, front_count.bit_length() - 1)

    def high_gather(*blocks):
        for bit in high_bits:
            received = traded(jnp.concatenate(blocks, 1), "front", 1 << bit)
            ends = [sum(b.shape[1] for b in blocks[: i + 1]) for i in range(len(blocks))]
            blocks = [
                ordered(b, received[:, end - b.shape[1] : end], front_id >> bit & 1, 1)
                for b, end in zip(blocks, ends)
            ]
        return blocks[0] if len(blocks) == 1 else blocks

    def high_scatter(block):
        for bit in reversed(high_bits):
            upper = front_id >> bit & 1
            block = part(block, upper, 2, 1).astype(F32) + traded(
                part(block, 1 - upper, 2, 1).astype(BF16), "front", 1 << bit
            ).astype(F32)
        return block

    def side_scatter(block):
        return part(block, side, 2, 1) + traded(
            part(block, 1 - side, 2, 1).astype(BF16), "leaf", 1
        ).astype(F32)

    def pair_forward(vector, own, other):
        return ordered(forward(vector, own), forward(vector, other), odd, 1).astype(BF16)

    def pair_adjoint(vector, own, other):
        return adjoint(part(vector, odd, 2, 1), own) + adjoint(part(vector, 1 - odd, 2, 1), other)

    def high_sum(block):
        for bit in high_bits:
            block = block + traded(block.astype(BF16), "front", 1 << bit).astype(F32)
        return block

    def pair_rows(block):
        return part(block, front_id // 2, front_count // 2, 1)

    def high_pieces(own):
        pieces = [own]
        for bit in high_bits:
            pieces += [traded(piece, "front", 1 << bit) for piece in pieces]
        return pieces

    def in_order(blocks, axis):
        for bit in range(front_count.bit_length() - 1):
            blocks = [
                ordered(blocks[i], blocks[i + 1], front_id >> bit & 1, axis)
                for i in range(0, len(blocks), 2)
            ]
        return blocks[0]

    def leaf_forward(vector, pieces):
        return in_order([forward(vector, piece) for piece in pieces], 1).astype(BF16)

    def leaf_adjoint(vector, pieces):
        return sum(
            adjoint(part(vector, front_id ^ i, front_count, 1), piece)
            for i, piece in enumerate(pieces)
        )

    def alternated(even, odd_ones):
        return [piece for pieces in zip(even, odd_ones) for piece in pieces]

    inverse0 = inverse_blocks[:, :leaf_rows]
    inverse1 = inverse_blocks[:, leaf_rows : 3 * leaf_rows]
    inverse2 = inverse_blocks[:, 3 * leaf_rows :]
    update0 = update_blocks[:, :leaf_rows]
    update1 = update_blocks[:, leaf_rows:]
    inverse0, inverse1, inverse2, update0, update1 = together(
        inverse0, inverse1, inverse2, update0, update1
    )

    lists = jnp.concatenate([asm_owner[:, :, 0], asm_row], 0).astype(BF16)
    lists = jnp.pad(lists, ((0, 4), (0, 2 * own_rows + LEVELS * half_cols - own_rows)))

    def parcel(mask):
        half = odd if mask % 2 == 0 else 1 - odd
        columns = [part(rhs[level], half, 2, 1) for level in range(LEVELS)]
        updates = part(update0, (front_id ^ mask) // 2, front_count // 2, 1)
        return jnp.concatenate([jnp.concatenate([updates, *columns], 1), lists], 0)

    parcels = {0: parcel(0)}
    for mask in sorted(range(1, front_count), key=lambda mask: (mask + 1) % front_count):
        parcels[mask] = traded(parcel(mask), "front", mask)
    parcels = [parcels[mask] for mask in range(front_count)]
    inverse0_pair = traded(inverse0, "front", 1)
    cores2 = [
        jnp.concatenate(
            [inverse2[:, (2 * other + core) * leaf_rows :][:, :leaf_rows] for other in range(2)], 1
        )
        for core in range(2)
    ]
    handed2 = jnp.where(side == 1, cores2[0], cores2[1])
    block2 = jnp.where(side == 1, cores2[1], cores2[0])
    block2 = jnp.concatenate([block2, traded(handed2, "leaf", 1)], 0)
    wing2 = traded(block2, "leaf", 2)
    inverse1_pair = traded(after(inverse1, inverse0_pair), "front", 1)
    *parcels, block2, inverse0_pair = together(*parcels, block2, inverse0_pair)
    update0_columns = in_order([block[:own_rows, : 2 * own_rows] for block in parcels], 0)

    def level_rows(blocks, level):
        return in_order(
            [
                block[:own_rows, 2 * own_rows + level * half_cols :][:, :half_cols]
                for block in blocks
            ],
            0,
        )

    rhs0 = level_rows(parcels, 0)

    solved0_pair = ordered(
        product(rhs0, inverse0, 0, 1), product(rhs0, inverse0_pair, 0, 1), odd, 1
    ).astype(BF16)
    update1_pair = traded(after(update1, solved0_pair), "front", 1)
    updated0 = forward(solved0_pair, update0_columns)
    parcels = together(*parcels, updated0)[:-1]
    rhs1, rhs2 = level_rows(parcels, 1).T, level_rows(parcels, 2).T
    lists = in_order([block[own_rows : own_rows + 4, :own_rows] for block in parcels], 1)
    lists_wing = traded(jnp.pad(lists, ((0, 12), (0, 0))), "leaf", 2)[:4]
    updated0 = high_sum(updated0).astype(BF16)
    updated0, inverse1_pair = together(updated0, inverse1_pair)

    def selector(lists, level_index):
        numbers = lists.astype(jnp.int32)
        target = numbers[level_index : level_index + 1] * own_rows + numbers[2 + level_index : 3 + level_index]
        return (jnp.arange(2 * leaf_rows)[:, None] == target).astype(BF16)

    select0 = selector(lists, 0)
    select1 = selector(lists, 1)
    pivots1 = ordered(rhs1, jnp.zeros_like(rhs1), side, 1).astype(F32) - forward(updated0, select0)
    pivots1 = (pivots1 + traded(pivots1.astype(BF16), "leaf", 1).astype(F32)).astype(BF16)

    solved1_pair = pair_forward(pivots1, inverse1, inverse1_pair)
    solved1 = high_gather(solved1_pair)
    solved1, update1_pair = together(solved1, update1_pair)
    solved1 = ordered(solved1, traded(solved1, "leaf", 1), side, 1)
    updated1_pair = pair_forward(solved1, update1, update1_pair)
    updated1 = high_gather(updated1_pair)
    updated1, wing2 = together(updated1, wing2)

    pivots2 = ordered(rhs2, jnp.zeros_like(rhs2), wing, 1).astype(F32) - forward(updated1, select1)
    pivots2 = (
        stacked(part(pivots2, wing, 2, 0))
        + traded(stacked(part(pivots2, 1 - wing, 2, 0)).astype(BF16), "leaf", 2).astype(F32)
    ).astype(BF16)
    pivots2 = jnp.concatenate(
        [
            jnp.concatenate(pieces, 0)
            for pieces in zip(flat(pivots2), flat(traded(pivots2, "front", 1)))
        ],
        0,
    )
    pivots2 = jnp.concatenate(flat(pivots2), 1)
    solved2 = [forward(pivots2, block2), forward(pivots2, wing2)]
    received = traded(jnp.concatenate(solved2, 1).astype(BF16), "leaf", 1)
    below2 = 0.0
    for index, block in enumerate((block2, wing2)):
        other = received[:, 2 * index * own_rows :][:, : 2 * own_rows]
        other = jnp.concatenate([other[:, own_rows:], other[:, :own_rows]], 1)
        below2 += adjoint((solved2[index] + other.astype(F32)).astype(BF16), block)
    handed2 = stacked(below2[quarter:].astype(BF16))
    below2 = stacked(below2[:quarter])
    below2 = (below2 + traded(handed2, "front", 1).astype(F32)).astype(BF16)

    def wing_gather(own, other):
        other = traded(stacked(other.astype(BF16)), "leaf", 2)
        return ordered(own.astype(BF16), jnp.concatenate(flat(other), 1), wing, 0)

    both2 = jnp.concatenate(flat(below2), 1)
    fetched1 = jnp.concatenate(
        [adjoint(both2, select1), adjoint(both2, selector(lists_wing, 1))], 0
    )
    fetched1 = high_scatter(fetched1)
    below2 = high_scatter(after(below2, fetched1))
    fetched1 = wing_gather(*flat(fetched1))
    carried1 = pair_adjoint(fetched1, update1, update1_pair)
    carried1 = side_scatter(carried1)
    carried1, below2 = together(carried1, below2)
    low2, high2 = flat(below2)
    solution2 = wing_gather(jnp.where(wing == 1, high2, low2), jnp.where(wing == 1, low2, high2))
    carried1, solution2 = together(high_scatter(carried1), solution2)
    weights1 = (solved1_pair.astype(F32) - carried1).astype(BF16)
    below1 = high_sum(side_scatter(pair_adjoint(weights1, inverse1, inverse1_pair))).astype(BF16)
    below1_all = ordered(below1, traded(below1, "leaf", 1), side, 1)

    fetched0 = adjoint(below1_all, select0).astype(BF16)
    weights0 = (solved0_pair.astype(F32) - adjoint(fetched0, update0_columns)).astype(BF16)
    below0 = pair_adjoint(weights0, inverse0, inverse0_pair)
    upper = jnp.concatenate([pair_rows(below1), solution2], 0)
    upper, below0 = together(upper, below0)
    upper_other = traded(part(upper, 1 - odd, 2, 1), "front", 1)
    shares = [
        traded(part(below0, front_id ^ mask, front_count, 1).astype(BF16), "front", mask)
        for mask in range(1, front_count)
    ]
    upper_other, *shares = together(upper_other, *shares)
    sums = [part(below0, front_id, front_count, 1), 0.0]
    for mask, share in enumerate(shares):
        sums[(mask + 1) % 2] += share.astype(F32)

    def finished(own, other):
        return ordered(own.astype(F32), other.astype(F32), odd, 0).T

    upper = part(upper, odd, 2, 1)
    return jnp.stack(
        [
            finished(*sums),
            finished(upper[:half_cols], upper_other[:half_cols]),
            finished(upper[half_cols:], upper_other[half_cols:]),
        ]
    )


def solution(mesh):
    placed = (
        P(None, ("leaf", "front"), None),
        P(("leaf", "front"), None),
        P(("leaf", "front"), None),
        P(None, ("leaf", "front"), None),
        P(None, ("leaf", "front")),
    )
    return jax.shard_map(
        shards,
        mesh=mesh,
        in_specs=placed,
        out_specs=P(None, ("leaf", "front"), None),
        check_vma=False,
    )
```

```python
import jax
import jax.numpy as jnp
from jax import lax
from jax.experimental.layout import Layout, with_layout_constraint
from jax.sharding import PartitionSpec as P

LEVELS = 3
BF16 = jnp.bfloat16
F32 = jnp.float32


def traded(shard, axis, mask):
    return lax.ppermute(shard, axis, [(i, i ^ mask) for i in range(lax.axis_size(axis))])


def product(left, right, left_dim, right_dim):
    return lax.dot_general(
        left, right, (((left_dim,), (right_dim,)), ((), ())), preferred_element_type=F32
    )


def forward(vector, matrix):
    return product(vector, matrix, 1, 1)


def adjoint(vector, matrix):
    return product(vector, matrix, 1, 0)


def ordered(own, other, upper, axis):
    return jnp.where(
        upper == 1,
        jnp.concatenate([other, own], axis),
        jnp.concatenate([own, other], axis),
    )


def by_rows(array):
    return with_layout_constraint(array, Layout(major_to_minor=(0, 1)))


def after(array, *earlier):
    return lax.optimization_barrier((array, *earlier))[0]


def together(*arrays):
    return lax.optimization_barrier(arrays)


def part(array, index, count, axis):
    size = array.shape[axis] // count
    return lax.dynamic_slice_in_dim(array, index * size, size, axis)


def stacked(block):
    middle = block.shape[1] // 2
    return jnp.concatenate([block[:, :middle], block[:, middle:]], 0)


def flat(block):
    middle = block.shape[0] // 2
    return block[:middle], block[middle:]


def shards(rhs, inverse_blocks, update_blocks, asm_owner, asm_row):
    own_rows, rhs_cols = rhs.shape[1:]
    front_count = lax.axis_size("front")
    leaf_rows = front_count * own_rows
    half_cols = rhs_cols // 2
    quarter = half_cols // 2
    leaf_id = lax.axis_index("leaf")
    front_id = lax.axis_index("front")
    odd = front_id % 2
    side = leaf_id % 2
    wing = leaf_id // 2 % 2
    high_bits = range(1, front_count.bit_length() - 1)

    def high_gather(*blocks):
        for bit in high_bits:
            received = traded(jnp.concatenate(blocks, 1), "front", 1 << bit)
            ends = [sum(b.shape[1] for b in blocks[: i + 1]) for i in range(len(blocks))]
            blocks = [
                ordered(b, received[:, end - b.shape[1] : end], front_id >> bit & 1, 1)
                for b, end in zip(blocks, ends)
            ]
        return blocks[0] if len(blocks) == 1 else blocks

    def high_scatter(block):
        for bit in reversed(high_bits):
            upper = front_id >> bit & 1
            block = part(block, upper, 2, 1).astype(F32) + traded(
                part(block, 1 - upper, 2, 1).astype(BF16), "front", 1 << bit
            ).astype(F32)
        return block

    def side_scatter(block):
        return part(block, side, 2, 1) + traded(
            part(block, 1 - side, 2, 1).astype(BF16), "leaf", 1
        ).astype(F32)

    def pair_forward(vector, own, other):
        return ordered(forward(vector, own), forward(vector, other), odd, 1).astype(BF16)

    def pair_adjoint(vector, own, other):
        return adjoint(part(vector, odd, 2, 1), own) + adjoint(part(vector, 1 - odd, 2, 1), other)

    def high_sum(block):
        for bit in high_bits:
            block = block + traded(block.astype(BF16), "front", 1 << bit).astype(F32)
        return block

    def pair_rows(block):
        return part(block, front_id // 2, front_count // 2, 1)

    def high_pieces(own):
        pieces = [own]
        for bit in high_bits:
            pieces += [traded(piece, "front", 1 << bit) for piece in pieces]
        return pieces

    def in_order(blocks, axis):
        for bit in range(front_count.bit_length() - 1):
            blocks = [
                ordered(blocks[i], blocks[i + 1], front_id >> bit & 1, axis)
                for i in range(0, len(blocks), 2)
            ]
        return blocks[0]

    def leaf_forward(vector, pieces):
        return in_order([forward(vector, piece) for piece in pieces], 1).astype(BF16)

    def leaf_adjoint(vector, pieces):
        return sum(
            adjoint(part(vector, front_id ^ i, front_count, 1), piece)
            for i, piece in enumerate(pieces)
        )

    def alternated(even, odd_ones):
        return [piece for pieces in zip(even, odd_ones) for piece in pieces]

    inverse0 = inverse_blocks[:, :leaf_rows]
    inverse1 = inverse_blocks[:, leaf_rows : 3 * leaf_rows]
    inverse2 = inverse_blocks[:, 3 * leaf_rows :]
    update0 = update_blocks[:, :leaf_rows]
    update1 = update_blocks[:, leaf_rows:]
    inverse0, inverse1, inverse2, update0, update1 = together(
        inverse0, inverse1, inverse2, update0, update1
    )

    lists = jnp.concatenate([asm_owner[:, :, 0], asm_row], 0).astype(BF16)
    lists = jnp.pad(lists, ((0, 4), (0, 2 * own_rows + LEVELS * half_cols - own_rows)))

    def parcel(mask):
        half = odd if mask % 2 == 0 else 1 - odd
        columns = [part(rhs[level], half, 2, 1) for level in range(LEVELS)]
        updates = part(update0, (front_id ^ mask) // 2, front_count // 2, 1)
        return by_rows(jnp.concatenate([jnp.concatenate([updates, *columns], 1), lists], 0))

    parcels = {0: parcel(0)}
    for mask in sorted(range(1, front_count), key=lambda mask: (mask + 1) % front_count):
        parcels[mask] = traded(parcel(mask), "front", mask)
    parcels = [parcels[mask] for mask in range(front_count)]
    cores1 = [update1[:, :leaf_rows], update1[:, leaf_rows:]]
    handed1 = jnp.where(side == 1, cores1[0], cores1[1])
    block1 = jnp.where(side == 1, cores1[1], cores1[0])
    block1 = jnp.concatenate([block1, traded(handed1, "leaf", 1)], 0)

    def pair_columns(mask):
        return part(block1, (front_id ^ mask) // 2, front_count // 2, 1)

    inverse0_pair = traded(inverse0, "front", 1)
    cores2 = [
        jnp.concatenate(
            [inverse2[:, (2 * other + core) * leaf_rows :][:, :leaf_rows] for other in range(2)], 1
        )
        for core in range(2)
    ]
    handed2 = jnp.where(side == 1, cores2[0], cores2[1])
    block2 = jnp.where(side == 1, cores2[1], cores2[0])
    block2 = jnp.concatenate([block2, traded(handed2, "leaf", 1)], 0)
    wing2 = traded(block2, "leaf", 2)
    inverse1_pair = traded(after(inverse1, inverse0_pair), "front", 1)
    columns1 = [pair_columns(0)] + [
        traded(pair_columns(mask), "front", mask) for mask in range(2, front_count, 2)
    ]
    *parcels, block2, inverse0_pair = together(*parcels, block2, inverse0_pair)
    parcels = [by_rows(block) for block in parcels]
    update0_columns = in_order([block[:own_rows, : 2 * own_rows] for block in parcels], 0)

    def level_rows(blocks, level):
        return in_order(
            [
                block[:own_rows, 2 * own_rows + level * half_cols :][:, :half_cols]
                for block in blocks
            ],
            0,
        )

    rhs0 = level_rows(parcels, 0)

    solved0_pair = ordered(
        product(rhs0, inverse0, 0, 1), product(rhs0, inverse0_pair, 0, 1), odd, 1
    ).astype(BF16)
    updated0 = forward(solved0_pair, update0_columns)
    parcels = together(*parcels, updated0)[:-1]
    rhs1, rhs2 = level_rows(parcels, 1).T, level_rows(parcels, 2).T
    lists = in_order([block[own_rows : own_rows + 4, :own_rows] for block in parcels], 1)
    columns1_near = traded(jnp.concatenate(columns1, 0), "front", 1)
    columns1 = alternated(
        columns1,
        [
            columns1_near[2 * i * own_rows : 2 * (i + 1) * own_rows]
            for i in range(len(columns1))
        ],
    )
    columns1_side = in_order([block[own_rows:] for block in columns1], 0)
    columns1 = in_order([block[:own_rows] for block in columns1], 0)
    updated0 = high_sum(updated0).astype(BF16)
    updated0, inverse1_pair = together(updated0, inverse1_pair)

    def selector(lists, level_index):
        numbers = lists.astype(jnp.int32)
        target = numbers[level_index : level_index + 1] * own_rows + numbers[2 + level_index : 3 + level_index]
        return (jnp.arange(2 * leaf_rows)[:, None] == target).astype(BF16)

    select0 = selector(lists, 0)
    select1 = selector(lists, 1)
    pivots1 = ordered(rhs1, jnp.zeros_like(rhs1), side, 1).astype(F32) - forward(updated0, select0)
    pivots1 = (pivots1 + traded(pivots1.astype(BF16), "leaf", 1).astype(F32)).astype(BF16)

    solved1_pair = pair_forward(pivots1, inverse1, inverse1_pair)
    updated1 = forward(solved1_pair, columns1_side).astype(BF16)
    updated1 = forward(solved1_pair, columns1) + traded(updated1, "leaf", 1).astype(F32)
    updated1 = high_sum(updated1).astype(BF16)
    updated1, wing2 = together(updated1, wing2)

    pivots2 = ordered(rhs2, jnp.zeros_like(rhs2), wing, 1).astype(F32) - forward(updated1, select1)
    pivots2 = (
        stacked(part(pivots2, wing, 2, 0))
        + traded(stacked(part(pivots2, 1 - wing, 2, 0)).astype(BF16), "leaf", 2).astype(F32)
    ).astype(BF16)
    pivots2 = jnp.concatenate(
        [
            jnp.concatenate(pieces, 0)
            for pieces in zip(flat(pivots2), flat(traded(pivots2, "front", 1)))
        ],
        0,
    )
    pivots2 = jnp.concatenate(flat(pivots2), 1)
    solved2 = [forward(pivots2, block2), forward(pivots2, wing2)]
    received = traded(jnp.concatenate(solved2, 1).astype(BF16), "leaf", 1)
    below2 = 0.0
    for index, block in enumerate((block2, wing2)):
        other = received[:, 2 * index * own_rows :][:, : 2 * own_rows]
        other = jnp.concatenate([other[:, own_rows:], other[:, :own_rows]], 1)
        below2 += adjoint((solved2[index] + other.astype(F32)).astype(BF16), block)
    handed2 = stacked(below2[quarter:].astype(BF16))
    below2 = stacked(below2[:quarter])
    below2 = below2 + traded(handed2, "front", 1).astype(F32)
    below2 = high_sum(below2).astype(BF16)
    own2 = flat(below2)
    other2 = flat(traded(below2, "leaf", 2))
    below2 = jnp.concatenate(
        [ordered(own, other, wing, 0) for own, other in zip(own2, other2)], 1
    )

    fetched1 = adjoint(below2, select1).astype(BF16)
    carried1 = adjoint(traded(fetched1, "leaf", 1), columns1_side) + adjoint(fetched1, columns1)
    weights1 = (solved1_pair.astype(F32) - carried1).astype(BF16)
    below1 = high_sum(side_scatter(pair_adjoint(weights1, inverse1, inverse1_pair))).astype(BF16)
    below1_all = ordered(below1, traded(below1, "leaf", 1), side, 1)

    fetched0 = adjoint(below1_all, select0).astype(BF16)
    weights0 = (solved0_pair.astype(F32) - adjoint(fetched0, update0_columns)).astype(BF16)
    below0 = pair_adjoint(weights0, inverse0, inverse0_pair)
    upper = jnp.concatenate([pair_rows(below1), pair_rows(part(below2, wing, 2, 1))], 0)
    upper, below0 = together(upper, below0)
    upper_other = traded(part(upper, 1 - odd, 2, 1), "front", 1)
    shares = [
        traded(part(below0, front_id ^ mask, front_count, 1).astype(BF16), "front", mask)
        for mask in range(1, front_count)
    ]
    upper_other, *shares = together(upper_other, *shares)
    sums = [part(below0, front_id, front_count, 1), 0.0]
    for mask, share in enumerate(shares):
        sums[(mask + 1) % 2] += share.astype(F32)

    def finished(own, other):
        return ordered(own.astype(F32), other.astype(F32), odd, 0).T

    upper = part(upper, odd, 2, 1)
    return jnp.stack(
        [
            finished(*sums),
            finished(upper[:half_cols], upper_other[:half_cols]),
            finished(upper[half_cols:], upper_other[half_cols:]),
        ]
    )


def solution(mesh):
    placed = (
        P(None, ("leaf", "front"), None),
        P(("leaf", "front"), None),
        P(("leaf", "front"), None),
        P(None, ("leaf", "front"), None),
        P(None, ("leaf", "front")),
    )
    return jax.shard_map(
        shards,
        mesh=mesh,
        in_specs=placed,
        out_specs=P(None, ("leaf", "front"), None),
        check_vma=False,
    )
```

```python
import jax
import jax.numpy as jnp
from jax import lax
from jax.experimental.layout import Layout, with_layout_constraint
from jax.sharding import PartitionSpec as P

LEVELS = 3
BF16 = jnp.bfloat16
F32 = jnp.float32


def traded(shard, axis, mask):
    return lax.ppermute(shard, axis, [(i, i ^ mask) for i in range(lax.axis_size(axis))])


def product(left, right, left_dim, right_dim):
    return lax.dot_general(
        left, right, (((left_dim,), (right_dim,)), ((), ())), preferred_element_type=F32
    )


def forward(vector, matrix):
    return product(vector, matrix, 1, 1)


def adjoint(vector, matrix):
    return product(vector, matrix, 1, 0)


def ordered(own, other, upper, axis):
    return jnp.where(
        upper == 1,
        jnp.concatenate([other, own], axis),
        jnp.concatenate([own, other], axis),
    )


def by_rows(array):
    return with_layout_constraint(array, Layout(major_to_minor=(0, 1)))


def after(array, *earlier):
    return lax.optimization_barrier((array, *earlier))[0]


def together(*arrays):
    return lax.optimization_barrier(arrays)


def part(array, index, count, axis):
    size = array.shape[axis] // count
    return lax.dynamic_slice_in_dim(array, index * size, size, axis)


def stacked(block):
    middle = block.shape[1] // 2
    return jnp.concatenate([block[:, :middle], block[:, middle:]], 0)


def flat(block):
    middle = block.shape[0] // 2
    return block[:middle], block[middle:]


def shards(rhs, inverse_blocks, update_blocks, asm_owner, asm_row):
    own_rows, rhs_cols = rhs.shape[1:]
    front_count = lax.axis_size("front")
    leaf_rows = front_count * own_rows
    half_cols = rhs_cols // 2
    quarter = half_cols // 2
    leaf_id = lax.axis_index("leaf")
    front_id = lax.axis_index("front")
    odd = front_id % 2
    side = leaf_id % 2
    wing = leaf_id // 2 % 2
    high_bits = range(1, front_count.bit_length() - 1)

    def high_gather(*blocks):
        for bit in high_bits:
            received = traded(jnp.concatenate(blocks, 1), "front", 1 << bit)
            ends = [sum(b.shape[1] for b in blocks[: i + 1]) for i in range(len(blocks))]
            blocks = [
                ordered(b, received[:, end - b.shape[1] : end], front_id >> bit & 1, 1)
                for b, end in zip(blocks, ends)
            ]
        return blocks[0] if len(blocks) == 1 else blocks

    def high_scatter(block):
        for bit in reversed(high_bits):
            upper = front_id >> bit & 1
            block = part(block, upper, 2, 1).astype(F32) + traded(
                part(block, 1 - upper, 2, 1).astype(BF16), "front", 1 << bit
            ).astype(F32)
        return block

    def side_scatter(block):
        return part(block, side, 2, 1) + traded(
            part(block, 1 - side, 2, 1).astype(BF16), "leaf", 1
        ).astype(F32)

    def pair_forward(vector, own, other):
        return ordered(forward(vector, own), forward(vector, other), odd, 1).astype(BF16)

    def pair_adjoint(vector, own, other):
        return adjoint(part(vector, odd, 2, 1), own) + adjoint(part(vector, 1 - odd, 2, 1), other)

    def high_sum(block):
        for bit in high_bits:
            block = block + traded(block.astype(BF16), "front", 1 << bit).astype(F32)
        return block

    def pair_rows(block):
        return part(block, front_id // 2, front_count // 2, 1)

    def high_pieces(own):
        pieces = [own]
        for bit in high_bits:
            pieces += [traded(piece, "front", 1 << bit) for piece in pieces]
        return pieces

    def in_order(blocks, axis):
        for bit in range(front_count.bit_length() - 1):
            blocks = [
                ordered(blocks[i], blocks[i + 1], front_id >> bit & 1, axis)
                for i in range(0, len(blocks), 2)
            ]
        return blocks[0]

    def leaf_forward(vector, pieces):
        return in_order([forward(vector, piece) for piece in pieces], 1).astype(BF16)

    def leaf_adjoint(vector, pieces):
        return sum(
            adjoint(part(vector, front_id ^ i, front_count, 1), piece)
            for i, piece in enumerate(pieces)
        )

    def alternated(even, odd_ones):
        return [piece for pieces in zip(even, odd_ones) for piece in pieces]

    inverse0 = inverse_blocks[:, :leaf_rows]
    inverse1 = inverse_blocks[:, leaf_rows : 3 * leaf_rows]
    inverse2 = inverse_blocks[:, 3 * leaf_rows :]
    update0 = update_blocks[:, :leaf_rows]
    update1 = update_blocks[:, leaf_rows:]
    inverse0, inverse1, inverse2, update0, update1 = together(
        inverse0, inverse1, inverse2, update0, update1
    )

    lists = jnp.concatenate([asm_owner[:, :, 0], asm_row], 0).astype(BF16)
    lists = jnp.pad(lists, ((0, 4), (0, 2 * own_rows + LEVELS * half_cols - own_rows)))

    def parcel(mask):
        half = odd if mask % 2 == 0 else 1 - odd
        columns = [part(rhs[level], half, 2, 1) for level in range(LEVELS)]
        updates = part(update0, (front_id ^ mask) // 2, front_count // 2, 1)
        return by_rows(jnp.concatenate([jnp.concatenate([updates, *columns], 1), lists], 0))

    parcels = {0: parcel(0)}
    for mask in sorted(range(1, front_count), key=lambda mask: (mask + 1) % front_count):
        parcels[mask] = traded(parcel(mask), "front", mask)
    parcels = [parcels[mask] for mask in range(front_count)]
    cores1 = [update1[:, :leaf_rows], update1[:, leaf_rows:]]
    handed1 = jnp.where(side == 1, cores1[0], cores1[1])
    block1 = jnp.where(side == 1, cores1[1], cores1[0])
    block1 = jnp.concatenate([block1, traded(handed1, "leaf", 1)], 0)

    def pair_columns(mask):
        return part(block1, (front_id ^ mask) // 2, front_count // 2, 1)

    inverse0_pair = traded(inverse0, "front", 1)
    inverse1_pair = traded(after(inverse1, inverse0_pair), "front", 1)
    columns1 = [pair_columns(0)] + [
        traded(pair_columns(mask), "front", mask) for mask in range(2, front_count, 2)
    ]
    *parcels, inverse0_pair = together(*parcels, inverse0_pair)
    parcels = [by_rows(block) for block in parcels]
    update0_columns = in_order([block[:own_rows, : 2 * own_rows] for block in parcels], 0)

    def level_rows(blocks, level):
        return in_order(
            [
                block[:own_rows, 2 * own_rows + level * half_cols :][:, :half_cols]
                for block in blocks
            ],
            0,
        )

    rhs0 = level_rows(parcels, 0)

    solved0_pair = ordered(
        product(rhs0, inverse0, 0, 1), product(rhs0, inverse0_pair, 0, 1), odd, 1
    ).astype(BF16)
    updated0 = forward(solved0_pair, update0_columns)
    cores2 = [
        jnp.concatenate(
            [inverse2[:, (2 * other + core) * leaf_rows :][:, :leaf_rows] for other in range(2)], 1
        )
        for core in range(2)
    ]
    cores2 = together(*cores2, solved0_pair)[:2]
    handed2 = jnp.where(side == 1, cores2[0], cores2[1])
    block2 = jnp.where(side == 1, cores2[1], cores2[0])
    block2 = jnp.concatenate([block2, traded(handed2, "leaf", 1)], 0)
    parcels = together(*parcels, updated0)[:-1]
    rhs1, rhs2 = level_rows(parcels, 1).T, level_rows(parcels, 2).T
    lists = in_order([block[own_rows : own_rows + 4, :own_rows] for block in parcels], 1)
    columns1_near = traded(after(jnp.concatenate(columns1, 0), updated0), "front", 1)
    columns1 = alternated(
        columns1,
        [
            columns1_near[2 * i * own_rows : 2 * (i + 1) * own_rows]
            for i in range(len(columns1))
        ],
    )
    columns1_side = in_order([block[own_rows:] for block in columns1], 0)
    columns1 = in_order([block[:own_rows] for block in columns1], 0)
    updated0 = high_sum(updated0).astype(BF16)
    updated0, inverse1_pair = together(updated0, inverse1_pair)
    wing2 = traded(after(block2, updated0), "leaf", 2)

    def selector(lists, level_index):
        numbers = lists.astype(jnp.int32)
        target = numbers[level_index : level_index + 1] * own_rows + numbers[2 + level_index : 3 + level_index]
        return (jnp.arange(2 * leaf_rows)[:, None] == target).astype(BF16)

    select0 = selector(lists, 0)
    select1 = selector(lists, 1)
    pivots1 = ordered(rhs1, jnp.zeros_like(rhs1), side, 1).astype(F32) - forward(updated0, select0)
    pivots1 = (pivots1 + traded(pivots1.astype(BF16), "leaf", 1).astype(F32)).astype(BF16)

    solved1_pair = pair_forward(pivots1, inverse1, inverse1_pair)
    updated1 = forward(solved1_pair, columns1_side).astype(BF16)
    updated1 = forward(solved1_pair, columns1) + traded(updated1, "leaf", 1).astype(F32)
    updated1 = high_sum(updated1).astype(BF16)
    updated1, wing2 = together(updated1, wing2)

    pivots2 = ordered(rhs2, jnp.zeros_like(rhs2), wing, 1).astype(F32) - forward(updated1, select1)
    pivots2 = (
        stacked(part(pivots2, wing, 2, 0))
        + traded(stacked(part(pivots2, 1 - wing, 2, 0)).astype(BF16), "leaf", 2).astype(F32)
    ).astype(BF16)
    pivots2 = jnp.concatenate(
        [
            jnp.concatenate(pieces, 0)
            for pieces in zip(flat(pivots2), flat(traded(pivots2, "front", 1)))
        ],
        0,
    )
    pivots2 = jnp.concatenate(flat(pivots2), 1)
    solved2 = [forward(pivots2, block2), forward(pivots2, wing2)]
    received = traded(jnp.concatenate(solved2, 1).astype(BF16), "leaf", 1)
    below2 = 0.0
    for index, block in enumerate((block2, wing2)):
        other = received[:, 2 * index * own_rows :][:, : 2 * own_rows]
        other = jnp.concatenate([other[:, own_rows:], other[:, :own_rows]], 1)
        below2 += adjoint((solved2[index] + other.astype(F32)).astype(BF16), block)
    handed2 = stacked(below2[quarter:].astype(BF16))
    below2 = stacked(below2[:quarter])
    below2 = below2 + traded(handed2, "front", 1).astype(F32)
    below2 = high_sum(below2).astype(BF16)
    own2 = flat(below2)
    other2 = flat(traded(below2, "leaf", 2))
    below2 = jnp.concatenate(
        [ordered(own, other, wing, 0) for own, other in zip(own2, other2)], 1
    )

    fetched1 = adjoint(below2, select1).astype(BF16)
    carried1 = adjoint(traded(fetched1, "leaf", 1), columns1_side) + adjoint(fetched1, columns1)
    weights1 = (solved1_pair.astype(F32) - carried1).astype(BF16)
    select0_late = lax.optimization_barrier(selector(after(lists, weights1), 0))
    below1 = high_sum(side_scatter(pair_adjoint(weights1, inverse1, inverse1_pair))).astype(BF16)
    below1_all = ordered(below1, traded(below1, "leaf", 1), side, 1)

    fetched0 = adjoint(below1_all, select0_late).astype(BF16)
    weights0 = (solved0_pair.astype(F32) - adjoint(fetched0, update0_columns)).astype(BF16)
    below0 = pair_adjoint(weights0, inverse0, inverse0_pair)
    upper = jnp.concatenate([pair_rows(below1), pair_rows(part(below2, wing, 2, 1))], 0)
    upper, below0 = together(upper, below0)
    upper_other = traded(part(upper, 1 - odd, 2, 1), "front", 1)
    shares = [
        traded(part(below0, front_id ^ mask, front_count, 1).astype(BF16), "front", mask)
        for mask in range(1, front_count)
    ]
    upper_other, *shares = together(upper_other, *shares)
    sums = [part(below0, front_id, front_count, 1), 0.0]
    for mask, share in enumerate(shares):
        sums[(mask + 1) % 2] += share.astype(F32)

    def finished(own, other):
        return ordered(own.astype(F32), other.astype(F32), odd, 0).T

    upper = part(upper, odd, 2, 1)
    return jnp.stack(
        [
            finished(*sums),
            finished(upper[:half_cols], upper_other[:half_cols]),
            finished(upper[half_cols:], upper_other[half_cols:]),
        ]
    )


def solution(mesh):
    placed = (
        P(None, ("leaf", "front"), None),
        P(("leaf", "front"), None),
        P(("leaf", "front"), None),
        P(None, ("leaf", "front"), None),
        P(None, ("leaf", "front")),
    )
    return jax.shard_map(
        shards,
        mesh=mesh,
        in_specs=placed,
        out_specs=P(None, ("leaf", "front"), None),
        check_vma=False,
    )
```

```python
import jax
import jax.numpy as jnp
from jax import lax
from jax.experimental.layout import Layout, with_layout_constraint
from jax.sharding import PartitionSpec as P

LEVELS = 3
BF16 = jnp.bfloat16
F32 = jnp.float32


def traded(shard, axis, mask):
    return lax.ppermute(shard, axis, [(i, i ^ mask) for i in range(lax.axis_size(axis))])


def product(left, right, left_dim, right_dim):
    return lax.dot_general(
        left, right, (((left_dim,), (right_dim,)), ((), ())), preferred_element_type=F32
    )


def forward(vector, matrix):
    return product(vector, matrix, 1, 1)


def adjoint(vector, matrix):
    return product(vector, matrix, 1, 0)


def ordered(own, other, upper, axis):
    return jnp.where(
        upper == 1,
        jnp.concatenate([other, own], axis),
        jnp.concatenate([own, other], axis),
    )


def by_rows(array):
    return with_layout_constraint(array, Layout(major_to_minor=(0, 1)))


def after(array, *earlier):
    return lax.optimization_barrier((array, *earlier))[0]


def together(*arrays):
    return lax.optimization_barrier(arrays)


def part(array, index, count, axis):
    size = array.shape[axis] // count
    return lax.dynamic_slice_in_dim(array, index * size, size, axis)


def stacked(block):
    middle = block.shape[1] // 2
    return jnp.concatenate([block[:, :middle], block[:, middle:]], 0)


def flat(block):
    middle = block.shape[0] // 2
    return block[:middle], block[middle:]


def shards(rhs, inverse_blocks, update_blocks, asm_owner, asm_row):
    own_rows, rhs_cols = rhs.shape[1:]
    front_count = lax.axis_size("front")
    leaf_rows = front_count * own_rows
    half_cols = rhs_cols // 2
    quarter = half_cols // 2
    leaf_id = lax.axis_index("leaf")
    front_id = lax.axis_index("front")
    odd = front_id % 2
    side = leaf_id % 2
    wing = leaf_id // 2 % 2
    high_bits = range(1, front_count.bit_length() - 1)

    def side_scatter(block):
        return part(block, side, 2, 1) + traded(
            part(block, 1 - side, 2, 1).astype(BF16), "leaf", 1
        ).astype(F32)

    def pair_forward(vector, own, other):
        return ordered(forward(vector, own), forward(vector, other), odd, 1).astype(BF16)

    def pair_adjoint(vector, own, other):
        return adjoint(part(vector, odd, 2, 1), own) + adjoint(part(vector, 1 - odd, 2, 1), other)

    def high_sum(block):
        for bit in high_bits:
            block = block + traded(block.astype(BF16), "front", 1 << bit).astype(F32)
        return block

    def pair_rows(block):
        return part(block, front_id // 2, front_count // 2, 1)

    def in_order(blocks, axis):
        for bit in range(front_count.bit_length() - 1):
            blocks = [
                ordered(blocks[i], blocks[i + 1], front_id >> bit & 1, axis)
                for i in range(0, len(blocks), 2)
            ]
        return blocks[0]

    def alternated(even, odd_ones):
        return [piece for pieces in zip(even, odd_ones) for piece in pieces]

    inverse0 = inverse_blocks[:, :leaf_rows]
    inverse1 = inverse_blocks[:, leaf_rows : 3 * leaf_rows]
    inverse2 = inverse_blocks[:, 3 * leaf_rows :]
    update0 = update_blocks[:, :leaf_rows]
    update1 = update_blocks[:, leaf_rows:]
    update0, inverse0, inverse1 = together(update0, inverse0, inverse1)
    inverse2, update1 = together(inverse2, update1)

    lists = jnp.concatenate([asm_owner[:, :, 0], asm_row], 0).astype(BF16)
    lists = jnp.pad(lists, ((0, 4), (0, 2 * own_rows + LEVELS * half_cols - own_rows)))

    def parcel(mask):
        half = odd if mask % 2 == 0 else 1 - odd
        columns = [part(rhs[level], half, 2, 1) for level in range(LEVELS)]
        updates = part(update0, (front_id ^ mask) // 2, front_count // 2, 1)
        return by_rows(jnp.concatenate([jnp.concatenate([updates, *columns], 1), lists], 0))

    parcels = {0: parcel(0)}
    for mask in sorted(range(1, front_count), key=lambda mask: (mask + 1) % front_count):
        parcels[mask] = traded(parcel(mask), "front", mask)
    parcels = [parcels[mask] for mask in range(front_count)]
    cores1 = [update1[:, :leaf_rows], update1[:, leaf_rows:]]
    handed1 = jnp.where(side == 1, cores1[0], cores1[1])
    block1 = jnp.where(side == 1, cores1[1], cores1[0])
    block1 = jnp.concatenate([block1, traded(handed1, "leaf", 1)], 0)

    def pair_columns(mask):
        return part(block1, (front_id ^ mask) // 2, front_count // 2, 1)

    inverse0_pair = traded(inverse0, "front", 1)
    inverse1_pair = traded(after(inverse1, inverse0_pair, block1), "front", 1)
    columns1 = [pair_columns(0)] + [
        traded(pair_columns(mask), "front", mask) for mask in range(2, front_count, 2)
    ]
    *parcels, inverse0_pair = together(*parcels, inverse0_pair)
    parcels = [by_rows(block) for block in parcels]
    update0_columns = in_order([block[:own_rows, : 2 * own_rows] for block in parcels], 0)

    def level_rows(blocks, level):
        return in_order(
            [
                block[:own_rows, 2 * own_rows + level * half_cols :][:, :half_cols]
                for block in blocks
            ],
            0,
        )

    rhs0 = level_rows(parcels, 0)

    solved0_pair = ordered(
        product(rhs0, inverse0, 0, 1), product(rhs0, inverse0_pair, 0, 1), odd, 1
    ).astype(BF16)
    updated0 = forward(solved0_pair, update0_columns)
    cores2 = [
        jnp.concatenate(
            [inverse2[:, (2 * other + core) * leaf_rows :][:, :leaf_rows] for other in range(2)], 1
        )
        for core in range(2)
    ]
    cores2 = together(*cores2, solved0_pair)[:2]
    handed2 = jnp.where(side == 1, cores2[0], cores2[1])
    block2 = jnp.where(side == 1, cores2[1], cores2[0])
    block2 = jnp.concatenate([block2, traded(handed2, "leaf", 1)], 0)
    parcels = together(*parcels, updated0)[:-1]
    rhs1, rhs2 = level_rows(parcels, 1).T, level_rows(parcels, 2).T
    lists = in_order([block[own_rows : own_rows + 4, :own_rows] for block in parcels], 1)
    columns1_near = traded(after(jnp.concatenate(columns1, 0), updated0), "front", 1)
    columns1 = alternated(
        columns1,
        [
            columns1_near[2 * i * own_rows : 2 * (i + 1) * own_rows]
            for i in range(len(columns1))
        ],
    )
    columns1_side = in_order([block[own_rows:] for block in columns1], 0)
    columns1 = in_order([block[:own_rows] for block in columns1], 0)
    updated0 = high_sum(updated0).astype(BF16)
    updated0, inverse1_pair = together(updated0, inverse1_pair)
    wing2 = traded(after(block2, updated0), "leaf", 2)

    def selector(lists, level_index):
        numbers = lists.astype(jnp.int32)
        target = numbers[level_index : level_index + 1] * own_rows + numbers[2 + level_index : 3 + level_index]
        return (jnp.arange(2 * leaf_rows)[:, None] == target).astype(BF16)

    select0 = selector(lists, 0)
    select1 = selector(lists, 1)
    pivots1 = ordered(rhs1, jnp.zeros_like(rhs1), side, 1).astype(F32) - forward(updated0, select0)
    pivots1 = (pivots1 + traded(pivots1.astype(BF16), "leaf", 1).astype(F32)).astype(BF16)

    solved1_pair = pair_forward(pivots1, inverse1, inverse1_pair)
    updated1 = forward(solved1_pair, columns1_side).astype(BF16)
    updated1 = forward(solved1_pair, columns1) + traded(updated1, "leaf", 1).astype(F32)
    updated1 = high_sum(updated1).astype(BF16)
    updated1, wing2 = together(updated1, wing2)

    pivots2 = ordered(rhs2, jnp.zeros_like(rhs2), wing, 1).astype(F32) - forward(updated1, select1)
    pivots2 = (
        stacked(part(pivots2, wing, 2, 0))
        + traded(stacked(part(pivots2, 1 - wing, 2, 0)).astype(BF16), "leaf", 2).astype(F32)
    ).astype(BF16)
    pivots2 = jnp.concatenate(
        [
            jnp.concatenate(pieces, 0)
            for pieces in zip(flat(pivots2), flat(traded(pivots2, "front", 1)))
        ],
        0,
    )
    pivots2 = jnp.concatenate(flat(pivots2), 1)
    solved2 = [forward(pivots2, block2), forward(pivots2, wing2)]
    received = traded(jnp.concatenate(solved2, 1).astype(BF16), "leaf", 1)
    below2 = 0.0
    for index, block in enumerate((block2, wing2)):
        other = received[:, 2 * index * own_rows :][:, : 2 * own_rows]
        other = jnp.concatenate([other[:, own_rows:], other[:, :own_rows]], 1)
        below2 += adjoint((solved2[index] + other.astype(F32)).astype(BF16), block)
    handed2 = stacked(below2[quarter:].astype(BF16))
    below2 = stacked(below2[:quarter])
    below2 = below2 + traded(handed2, "front", 1).astype(F32)
    select1_late = lax.optimization_barrier(selector(after(lists, below2), 1))
    below2 = high_sum(below2).astype(BF16)
    own2 = flat(below2)
    other2 = flat(traded(below2, "leaf", 2))
    below2 = jnp.concatenate(
        [ordered(own, other, wing, 0) for own, other in zip(own2, other2)], 1
    )

    fetched1 = adjoint(below2, select1_late).astype(BF16)
    carried1 = adjoint(traded(fetched1, "leaf", 1), columns1_side) + adjoint(fetched1, columns1)
    weights1 = (solved1_pair.astype(F32) - carried1).astype(BF16)
    select0_late = lax.optimization_barrier(selector(after(lists, weights1), 0))
    below1 = high_sum(side_scatter(pair_adjoint(weights1, inverse1, inverse1_pair))).astype(BF16)
    below1_all = ordered(below1, traded(below1, "leaf", 1), side, 1)

    fetched0 = adjoint(below1_all, select0_late).astype(BF16)
    weights0 = (solved0_pair.astype(F32) - adjoint(fetched0, update0_columns)).astype(BF16)
    below0 = pair_adjoint(weights0, inverse0, inverse0_pair)
    upper = jnp.concatenate([pair_rows(below1), pair_rows(part(below2, wing, 2, 1))], 0)
    upper, below0 = together(upper, below0)
    upper_other = traded(part(upper, 1 - odd, 2, 1), "front", 1)
    shares = [
        traded(part(below0, front_id ^ mask, front_count, 1).astype(BF16), "front", mask)
        for mask in range(1, front_count)
    ]
    upper_other, *shares = together(upper_other, *shares)
    sums = [part(below0, front_id, front_count, 1), 0.0]
    for mask, share in enumerate(shares):
        sums[(mask + 1) % 2] += share.astype(F32)

    def finished(own, other):
        return ordered(own.astype(F32), other.astype(F32), odd, 0).T

    upper = part(upper, odd, 2, 1)
    return jnp.stack(
        [
            finished(*sums),
            finished(upper[:half_cols], upper_other[:half_cols]),
            finished(upper[half_cols:], upper_other[half_cols:]),
        ]
    )


def solution(mesh):
    placed = (
        P(None, ("leaf", "front"), None),
        P(("leaf", "front"), None),
        P(("leaf", "front"), None),
        P(None, ("leaf", "front"), None),
        P(None, ("leaf", "front")),
    )
    return jax.shard_map(
        shards,
        mesh=mesh,
        in_specs=placed,
        out_specs=P(None, ("leaf", "front"), None),
        check_vma=False,
    )
```

```python
import jax
import jax.numpy as jnp
from jax import lax
from jax.experimental.layout import Layout, with_layout_constraint
from jax.sharding import PartitionSpec as P

LEVELS = 3
BF16 = jnp.bfloat16
F32 = jnp.float32


def traded(shard, axis, mask):
    return lax.ppermute(shard, axis, [(i, i ^ mask) for i in range(lax.axis_size(axis))])


def product(left, right, left_dim, right_dim):
    return lax.dot_general(
        left, right, (((left_dim,), (right_dim,)), ((), ())), preferred_element_type=F32
    )


def forward(vector, matrix):
    return product(vector, matrix, 1, 1)


def adjoint(vector, matrix):
    return product(vector, matrix, 1, 0)


def ordered(own, other, upper, axis):
    return jnp.where(
        upper == 1,
        jnp.concatenate([other, own], axis),
        jnp.concatenate([own, other], axis),
    )


def by_rows(array):
    return with_layout_constraint(array, Layout(major_to_minor=(0, 1)))


def after(array, *earlier):
    return lax.optimization_barrier((array, *earlier))[0]


def together(*arrays):
    return lax.optimization_barrier(arrays)


def part(array, index, count, axis):
    size = array.shape[axis] // count
    return lax.dynamic_slice_in_dim(array, index * size, size, axis)


def stacked(block):
    middle = block.shape[1] // 2
    return jnp.concatenate([block[:, :middle], block[:, middle:]], 0)


def flat(block):
    middle = block.shape[0] // 2
    return block[:middle], block[middle:]


def shards(rhs, inverse_blocks, update_blocks, asm_owner, asm_row):
    own_rows, rhs_cols = rhs.shape[1:]
    front_count = lax.axis_size("front")
    leaf_rows = front_count * own_rows
    half_cols = rhs_cols // 2
    quarter = half_cols // 2
    leaf_id = lax.axis_index("leaf")
    front_id = lax.axis_index("front")
    odd = front_id % 2
    side = leaf_id % 2
    wing = leaf_id // 2 % 2
    high_bits = range(1, front_count.bit_length() - 1)

    def side_scatter(block):
        return part(block, side, 2, 1) + traded(
            part(block, 1 - side, 2, 1).astype(BF16), "leaf", 1
        ).astype(F32)

    def pair_forward(vector, own, other):
        return ordered(forward(vector, own), forward(vector, other), odd, 1).astype(BF16)

    def pair_adjoint(vector, own, other):
        return adjoint(part(vector, odd, 2, 1), own) + adjoint(part(vector, 1 - odd, 2, 1), other)

    def high_sum(block):
        for bit in high_bits:
            block = block + traded(block.astype(BF16), "front", 1 << bit).astype(F32)
        return block

    def pair_rows(block):
        return part(block, front_id // 2, front_count // 2, 1)

    def in_order(blocks, axis):
        for bit in range(front_count.bit_length() - 1):
            blocks = [
                ordered(blocks[i], blocks[i + 1], front_id >> bit & 1, axis)
                for i in range(0, len(blocks), 2)
            ]
        return blocks[0]

    def alternated(even, odd_ones):
        return [piece for pieces in zip(even, odd_ones) for piece in pieces]

    inverse0 = inverse_blocks[:, :leaf_rows]
    inverse1 = inverse_blocks[:, leaf_rows : 3 * leaf_rows]
    inverse2 = inverse_blocks[:, 3 * leaf_rows :]
    update0 = update_blocks[:, :leaf_rows]
    update1 = update_blocks[:, leaf_rows:]
    update0, inverse0, inverse1 = together(update0, inverse0, inverse1)
    inverse2, update1 = together(inverse2, update1)

    lists = jnp.concatenate([asm_owner[:, :, 0], asm_row], 0).astype(BF16)
    lists = jnp.pad(lists, ((0, 4), (0, 2 * own_rows + LEVELS * half_cols - own_rows)))

    def parcel(mask):
        half = odd if mask % 2 == 0 else 1 - odd
        columns = [part(rhs[level], half, 2, 1) for level in range(LEVELS)]
        updates = part(update0, (front_id ^ mask) // 2, front_count // 2, 1)
        return by_rows(jnp.concatenate([jnp.concatenate([updates, *columns], 1), lists], 0))

    parcels = {0: parcel(0)}
    for mask in sorted(range(1, front_count), key=lambda mask: (mask + 2) % front_count):
        parcels[mask] = traded(parcel(mask), "front", mask)
    parcels = [parcels[mask] for mask in range(front_count)]
    cores1 = [update1[:, :leaf_rows], update1[:, leaf_rows:]]
    handed1 = jnp.where(side == 1, cores1[0], cores1[1])
    block1 = jnp.where(side == 1, cores1[1], cores1[0])
    block1 = jnp.concatenate([block1, traded(handed1, "leaf", 1)], 0)

    def pair_columns(mask):
        return part(block1, (front_id ^ mask) // 2, front_count // 2, 1)

    inverse0_pair = traded(inverse0, "front", 1)
    inverse1_pair = traded(after(inverse1, inverse0_pair, block1), "front", 1)
    columns1 = [pair_columns(0)] + [
        traded(pair_columns(mask), "front", mask) for mask in range(2, front_count, 2)
    ]
    *parcels, inverse0_pair = together(*parcels, inverse0_pair)
    parcels = [by_rows(block) for block in parcels]
    update0_columns = in_order([block[:own_rows, : 2 * own_rows] for block in parcels], 0)

    def level_rows(blocks, level):
        return in_order(
            [
                block[:own_rows, 2 * own_rows + level * half_cols :][:, :half_cols]
                for block in blocks
            ],
            0,
        )

    rhs0 = level_rows(parcels, 0)

    solved0_pair = ordered(
        product(rhs0, inverse0, 0, 1), product(rhs0, inverse0_pair, 0, 1), odd, 1
    ).astype(BF16)
    updated0 = forward(solved0_pair, update0_columns)
    cores2 = [
        jnp.concatenate(
            [inverse2[:, (2 * other + core) * leaf_rows :][:, :leaf_rows] for other in range(2)], 1
        )
        for core in range(2)
    ]
    cores2 = together(*cores2, solved0_pair)[:2]
    handed2 = jnp.where(side == 1, cores2[0], cores2[1])
    block2 = jnp.where(side == 1, cores2[1], cores2[0])
    block2 = jnp.concatenate([block2, traded(handed2, "leaf", 1)], 0)
    parcels = together(*parcels, updated0)[:-1]
    rhs1, rhs2 = level_rows(parcels, 1).T, level_rows(parcels, 2).T
    lists = in_order([block[own_rows : own_rows + 4, :own_rows] for block in parcels], 1)
    columns1_near = traded(after(jnp.concatenate(columns1, 0), updated0), "front", 1)
    columns1 = alternated(
        columns1,
        [
            columns1_near[2 * i * own_rows : 2 * (i + 1) * own_rows]
            for i in range(len(columns1))
        ],
    )
    columns1_side = in_order([block[own_rows:] for block in columns1], 0)
    columns1 = in_order([block[:own_rows] for block in columns1], 0)
    updated0 = high_sum(updated0).astype(BF16)
    updated0, inverse1_pair = together(updated0, inverse1_pair)
    wing2 = traded(after(block2, updated0), "leaf", 2)

    def selector(lists, level_index):
        numbers = lists.astype(jnp.int32)
        target = numbers[level_index : level_index + 1] * own_rows + numbers[2 + level_index : 3 + level_index]
        return (jnp.arange(2 * leaf_rows)[:, None] == target).astype(BF16)

    select0 = selector(lists, 0)
    select1 = selector(lists, 1)
    pivots1 = ordered(rhs1, jnp.zeros_like(rhs1), side, 1).astype(F32) - forward(updated0, select0)
    pivots1 = (pivots1 + traded(pivots1.astype(BF16), "leaf", 1).astype(F32)).astype(BF16)

    solved1_pair = pair_forward(pivots1, inverse1, inverse1_pair)
    updated1 = forward(solved1_pair, columns1_side).astype(BF16)
    updated1 = forward(solved1_pair, columns1) + traded(updated1, "leaf", 1).astype(F32)
    updated1 = high_sum(updated1).astype(BF16)
    updated1, wing2 = together(updated1, wing2)

    pivots2 = ordered(rhs2, jnp.zeros_like(rhs2), wing, 1).astype(F32) - forward(updated1, select1)
    pivots2 = (
        stacked(part(pivots2, wing, 2, 0))
        + traded(stacked(part(pivots2, 1 - wing, 2, 0)).astype(BF16), "leaf", 2).astype(F32)
    ).astype(BF16)
    pivots2 = jnp.concatenate(
        [
            jnp.concatenate(pieces, 0)
            for pieces in zip(flat(pivots2), flat(traded(pivots2, "front", 1)))
        ],
        0,
    )
    pivots2 = jnp.concatenate(flat(pivots2), 1)
    solved2 = [forward(pivots2, block2), forward(pivots2, wing2)]
    received = traded(jnp.concatenate(solved2, 1).astype(BF16), "leaf", 1)
    below2 = 0.0
    for index, block in enumerate((block2, wing2)):
        other = received[:, 2 * index * own_rows :][:, : 2 * own_rows]
        other = jnp.concatenate([other[:, own_rows:], other[:, :own_rows]], 1)
        below2 += adjoint((solved2[index] + other.astype(F32)).astype(BF16), block)
    handed2 = stacked(below2[quarter:].astype(BF16))
    below2 = stacked(below2[:quarter])
    below2 = below2 + traded(handed2, "front", 1).astype(F32)
    select1_late = lax.optimization_barrier(selector(after(lists, below2), 1))
    below2 = high_sum(below2).astype(BF16)
    own2 = flat(below2)
    other2 = flat(traded(below2, "leaf", 2))
    below2 = jnp.concatenate(
        [ordered(own, other, wing, 0) for own, other in zip(own2, other2)], 1
    )

    fetched1 = adjoint(below2, select1_late).astype(BF16)
    carried1 = adjoint(traded(fetched1, "leaf", 1), columns1_side) + adjoint(fetched1, columns1)
    weights1 = (solved1_pair.astype(F32) - carried1).astype(BF16)
    select0_late = lax.optimization_barrier(selector(after(lists, weights1), 0))
    below1 = high_sum(side_scatter(pair_adjoint(weights1, inverse1, inverse1_pair))).astype(BF16)
    below1_all = ordered(below1, traded(below1, "leaf", 1), side, 1)

    fetched0 = adjoint(below1_all, select0_late).astype(BF16)
    weights0 = (solved0_pair.astype(F32) - adjoint(fetched0, update0_columns)).astype(BF16)
    below0 = pair_adjoint(weights0, inverse0, inverse0_pair)
    upper = jnp.concatenate([pair_rows(below1), pair_rows(part(below2, wing, 2, 1))], 0)
    upper, below0 = together(upper, below0)
    upper_other = traded(part(upper, 1 - odd, 2, 1), "front", 1)
    shares = [
        traded(part(below0, front_id ^ mask, front_count, 1).astype(BF16), "front", mask)
        for mask in range(1, front_count)
    ]
    upper_other, *shares = together(upper_other, *shares)
    sums = [part(below0, front_id, front_count, 1), 0.0]
    for mask, share in enumerate(shares):
        sums[(mask + 1) % 2] += share.astype(F32)

    def finished(own, other):
        return ordered(own.astype(F32), other.astype(F32), odd, 0).T

    upper = part(upper, odd, 2, 1)
    return jnp.stack(
        [
            finished(*sums),
            finished(upper[:half_cols], upper_other[:half_cols]),
            finished(upper[half_cols:], upper_other[half_cols:]),
        ]
    )


def solution(mesh):
    placed = (
        P(None, ("leaf", "front"), None),
        P(("leaf", "front"), None),
        P(("leaf", "front"), None),
        P(None, ("leaf", "front"), None),
        P(None, ("leaf", "front")),
    )
    return jax.shard_map(
        shards,
        mesh=mesh,
        in_specs=placed,
        out_specs=P(None, ("leaf", "front"), None),
        check_vma=False,
    )
```

```python
import jax
import jax.numpy as jnp
from jax import lax
from jax.experimental.layout import Layout, with_layout_constraint
from jax.sharding import PartitionSpec as P

LEVELS = 3
BF16 = jnp.bfloat16
F32 = jnp.float32


def traded(shard, axis, mask):
    return lax.ppermute(shard, axis, [(i, i ^ mask) for i in range(lax.axis_size(axis))])


def product(left, right, left_dim, right_dim):
    return lax.dot_general(
        left, right, (((left_dim,), (right_dim,)), ((), ())), preferred_element_type=F32
    )


def forward(vector, matrix):
    return product(vector, matrix, 1, 1)


def adjoint(vector, matrix):
    return product(vector, matrix, 1, 0)


def ordered(own, other, upper, axis):
    return jnp.where(
        upper == 1,
        jnp.concatenate([other, own], axis),
        jnp.concatenate([own, other], axis),
    )


def by_rows(array):
    return with_layout_constraint(array, Layout(major_to_minor=(0, 1)))


def after(array, *earlier):
    return lax.optimization_barrier((array, *earlier))[0]


def together(*arrays):
    return lax.optimization_barrier(arrays)


def part(array, index, count, axis):
    size = array.shape[axis] // count
    return lax.dynamic_slice_in_dim(array, index * size, size, axis)


def stacked(block):
    middle = block.shape[1] // 2
    return jnp.concatenate([block[:, :middle], block[:, middle:]], 0)


def flat(block):
    middle = block.shape[0] // 2
    return block[:middle], block[middle:]


def shards(rhs, inverse_blocks, update_blocks, asm_owner, asm_row):
    own_rows, rhs_cols = rhs.shape[1:]
    front_count = lax.axis_size("front")
    leaf_rows = front_count * own_rows
    half_cols = rhs_cols // 2
    quarter = half_cols // 2
    leaf_id = lax.axis_index("leaf")
    front_id = lax.axis_index("front")
    odd = front_id % 2
    side = leaf_id % 2
    wing = leaf_id // 2 % 2
    high_bits = range(1, front_count.bit_length() - 1)

    def side_scatter(block):
        return part(block, side, 2, 1) + traded(
            part(block, 1 - side, 2, 1).astype(BF16), "leaf", 1
        ).astype(F32)

    def pair_forward(vector, own, other):
        return ordered(forward(vector, own), forward(vector, other), odd, 1).astype(BF16)

    def pair_adjoint(vector, own, other):
        return adjoint(part(vector, odd, 2, 1), own) + adjoint(part(vector, 1 - odd, 2, 1), other)

    def high_sum(block):
        for bit in high_bits:
            block = block + traded(block.astype(BF16), "front", 1 << bit).astype(F32)
        return block

    def pair_rows(block):
        return part(block, front_id // 2, front_count // 2, 1)

    def in_order(blocks, axis):
        for bit in range(front_count.bit_length() - 1):
            blocks = [
                ordered(blocks[i], blocks[i + 1], front_id >> bit & 1, axis)
                for i in range(0, len(blocks), 2)
            ]
        return blocks[0]

    def alternated(even, odd_ones):
        return [piece for pieces in zip(even, odd_ones) for piece in pieces]

    inverse0 = inverse_blocks[:, :leaf_rows]
    inverse1 = inverse_blocks[:, leaf_rows : 3 * leaf_rows]
    inverse2 = inverse_blocks[:, 3 * leaf_rows :]
    update0 = update_blocks[:, :leaf_rows]
    update1 = update_blocks[:, leaf_rows:]
    update0, inverse0, inverse1 = together(update0, inverse0, inverse1)
    inverse2, update1 = together(inverse2, update1)

    lists = jnp.concatenate([asm_owner[:, :, 0], asm_row], 0).astype(BF16)
    lists = jnp.pad(lists, ((0, 4), (0, 2 * own_rows + LEVELS * half_cols - own_rows)))

    def parcel(mask):
        half = odd if mask % 2 == 0 else 1 - odd
        columns = [part(rhs[level], half, 2, 1) for level in range(LEVELS)]
        updates = part(update0, (front_id ^ mask) // 2, front_count // 2, 1)
        return by_rows(jnp.concatenate([jnp.concatenate([updates, *columns], 1), lists], 0))

    parcels = {0: parcel(0)}
    for mask in sorted(range(1, front_count), key=lambda mask: (mask + 2) % front_count):
        parcels[mask] = traded(parcel(mask), "front", mask)
    parcels = [parcels[mask] for mask in range(front_count)]
    cores1 = [update1[:, :leaf_rows], update1[:, leaf_rows:]]
    handed1 = jnp.where(side == 1, cores1[0], cores1[1])
    block1 = jnp.where(side == 1, cores1[1], cores1[0])
    block1 = jnp.concatenate([block1, traded(handed1, "leaf", 1)], 0)

    def pair_columns(mask):
        return part(block1, (front_id ^ mask) // 2, front_count // 2, 1)

    inverse0_pair = traded(inverse0, "front", 1)
    inverse1_pair = traded(after(inverse1, inverse0_pair, block1), "front", 1)
    columns1 = [pair_columns(0)] + [
        traded(pair_columns(mask), "front", mask) for mask in range(2, front_count, 2)
    ]
    *parcels, inverse0_pair = together(*parcels, inverse0_pair)
    parcels = [by_rows(block) for block in parcels]
    update0_columns = in_order([block[:own_rows, : 2 * own_rows] for block in parcels], 0)

    def level_rows(blocks, level):
        return in_order(
            [
                block[:own_rows, 2 * own_rows + level * half_cols :][:, :half_cols]
                for block in blocks
            ],
            0,
        )

    rhs0 = level_rows(parcels, 0)

    solved0_pair = ordered(
        product(rhs0, inverse0, 0, 1), product(rhs0, inverse0_pair, 0, 1), odd, 1
    ).astype(BF16)
    updated0 = forward(solved0_pair, update0_columns)
    cores2 = [
        jnp.concatenate(
            [inverse2[:, (2 * other + core) * leaf_rows :][:, :leaf_rows] for other in range(2)], 1
        )
        for core in range(2)
    ]
    cores2 = together(*cores2, solved0_pair)[:2]
    handed2 = jnp.where(side == 1, cores2[0], cores2[1])
    block2 = jnp.where(side == 1, cores2[1], cores2[0])
    block2 = jnp.concatenate([block2, traded(handed2, "leaf", 1)], 0)
    parcels = together(*parcels, updated0)[:-1]
    rhs1, rhs2 = level_rows(parcels, 1).T, level_rows(parcels, 2).T
    lists = in_order([block[own_rows : own_rows + 4, :own_rows] for block in parcels], 1)
    columns1_near = traded(after(jnp.concatenate(columns1, 0), updated0), "front", 1)
    columns1 = alternated(
        columns1,
        [
            columns1_near[2 * i * own_rows : 2 * (i + 1) * own_rows]
            for i in range(len(columns1))
        ],
    )
    columns1_side = in_order([block[own_rows:] for block in columns1], 0)
    columns1 = in_order([block[:own_rows] for block in columns1], 0)
    updated0 = high_sum(updated0).astype(BF16)
    updated0, inverse1_pair = together(updated0, inverse1_pair)
    wing2 = traded(after(block2, updated0), "leaf", 2)

    def selector(lists, level_index):
        numbers = lists.astype(jnp.int32)
        target = numbers[level_index : level_index + 1] * own_rows + numbers[2 + level_index : 3 + level_index]
        return (jnp.arange(2 * leaf_rows)[:, None] == target).astype(BF16)

    select0 = selector(lists, 0)
    pivots1 = ordered(rhs1, jnp.zeros_like(rhs1), side, 1).astype(F32) - forward(updated0, select0)
    pivots1 = (pivots1 + traded(pivots1.astype(BF16), "leaf", 1).astype(F32)).astype(BF16)

    solved1_pair = pair_forward(pivots1, inverse1, inverse1_pair)
    updated1 = forward(solved1_pair, columns1_side).astype(BF16)
    updated1 = forward(solved1_pair, columns1) + traded(updated1, "leaf", 1).astype(F32)
    select1 = lax.optimization_barrier(selector(after(lists, solved1_pair), 1))
    updated1 = high_sum(updated1).astype(BF16)
    updated1, wing2 = together(updated1, wing2)

    pivots2 = ordered(rhs2, jnp.zeros_like(rhs2), wing, 1).astype(F32) - forward(updated1, select1)
    pivots2 = (
        stacked(part(pivots2, wing, 2, 0))
        + traded(stacked(part(pivots2, 1 - wing, 2, 0)).astype(BF16), "leaf", 2).astype(F32)
    ).astype(BF16)
    pivots2 = jnp.concatenate(
        [
            jnp.concatenate(pieces, 0)
            for pieces in zip(flat(pivots2), flat(traded(pivots2, "front", 1)))
        ],
        0,
    )
    pivots2 = jnp.concatenate(flat(pivots2), 1)
    solved2 = [forward(pivots2, block2), forward(pivots2, wing2)]
    received = traded(jnp.concatenate(solved2, 1).astype(BF16), "leaf", 1)
    below2 = 0.0
    for index, block in enumerate((block2, wing2)):
        other = received[:, 2 * index * own_rows :][:, : 2 * own_rows]
        other = jnp.concatenate([other[:, own_rows:], other[:, :own_rows]], 1)
        below2 += adjoint((solved2[index] + other.astype(F32)).astype(BF16), block)
    handed2 = stacked(below2[quarter:].astype(BF16))
    below2 = stacked(below2[:quarter])
    below2 = below2 + traded(handed2, "front", 1).astype(F32)
    select1_late = lax.optimization_barrier(selector(after(lists, below2), 1))
    below2 = high_sum(below2).astype(BF16)
    own2 = flat(below2)
    other2 = flat(traded(below2, "leaf", 2))
    below2 = jnp.concatenate(
        [ordered(own, other, wing, 0) for own, other in zip(own2, other2)], 1
    )

    fetched1 = adjoint(below2, select1_late).astype(BF16)
    carried1 = adjoint(traded(fetched1, "leaf", 1), columns1_side) + adjoint(fetched1, columns1)
    weights1 = (solved1_pair.astype(F32) - carried1).astype(BF16)
    select0_late = lax.optimization_barrier(selector(after(lists, weights1), 0))
    below1 = high_sum(side_scatter(pair_adjoint(weights1, inverse1, inverse1_pair))).astype(BF16)
    below1_all = ordered(below1, traded(below1, "leaf", 1), side, 1)

    fetched0 = adjoint(below1_all, select0_late).astype(BF16)
    weights0 = (solved0_pair.astype(F32) - adjoint(fetched0, update0_columns)).astype(BF16)
    below0 = pair_adjoint(weights0, inverse0, inverse0_pair)
    upper = jnp.concatenate([pair_rows(below1), pair_rows(part(below2, wing, 2, 1))], 0)
    upper, below0 = together(upper, below0)
    upper_other = traded(part(upper, 1 - odd, 2, 1), "front", 1)
    shares = [
        traded(part(below0, front_id ^ mask, front_count, 1).astype(BF16), "front", mask)
        for mask in range(1, front_count)
    ]
    upper_other, *shares = together(upper_other, *shares)
    sums = [part(below0, front_id, front_count, 1), 0.0]
    for mask, share in enumerate(shares):
        sums[(mask + 1) % 2] += share.astype(F32)

    def finished(own, other):
        return ordered(own.astype(F32), other.astype(F32), odd, 0).T

    upper = part(upper, odd, 2, 1)
    return jnp.stack(
        [
            finished(*sums),
            finished(upper[:half_cols], upper_other[:half_cols]),
            finished(upper[half_cols:], upper_other[half_cols:]),
        ]
    )


def solution(mesh):
    placed = (
        P(None, ("leaf", "front"), None),
        P(("leaf", "front"), None),
        P(("leaf", "front"), None),
        P(None, ("leaf", "front"), None),
        P(None, ("leaf", "front")),
    )
    return jax.shard_map(
        shards,
        mesh=mesh,
        in_specs=placed,
        out_specs=P(None, ("leaf", "front"), None),
        check_vma=False,
    )
```
